32 devices in a mesh: orbit: 2 (over y), lon: 4 (over z), lat: 4 (over x, core).
Axes of the slice: x: 2, y: 2, z: 4, core: 2. Of those that a mesh axis runs over, the one named last changes fastest.
Arguments:
- kernel: float32 [20, 131072], P(None, ('orbit', 'lon', 'lat')), may hold values from 0.2 to 1.2
- residual: float32 [131072], P(('orbit', 'lon', 'lat')), may hold values from -6 to 6
- owner_block: int32 [131072, 1], P(('orbit', 'lon', 'lat')), may hold values from 0 to 15; in each aligned block of 4096 rows (0 to 4095, 4096 to 8191, ...) at most 1024 rows name the same one
- column: int32 [131072], P(('orbit', 'lon', 'lat')), may hold values from 0 to 1023
- time_step: int32 [131072], P(('orbit', 'lon', 'lat')), may hold values from 0 to 7
- horizontal: float32 [4, 72, 32, 512], P(None, None, 'lon', 'lat'), may hold values from 0.04 to 0.22
- vertical: float32 [71, 32, 512], P(None, 'lon', 'lat'), may hold values from 0.02 to 0.24
Outputs:
- adjoint_state: float32 [72, 32, 512], P(None, 'lon', 'lat')
- flux_gradient: float32 [32, 512], P('lon', 'lat')
The draws below stay inside these ranges and needn't reach their ends.
Inputs may be any that keep to these rules, and one draw needn't show every extreme that they name: `owner_block`: among the soundings of one device no block is named more than 1024 times, and in some device's soundings one block is named exactly 1024 times.
All inputs are finite; a program needn't handle non-finite values.
Results may differ from the reference program's by a relative error of at most 0.0001.
Values sent between devices are 32-bit elements; how exact they have to be, the bound alone decides.
A program may use at most 128 MiB of HBM per device.

```python
import math
import jax
import jax.numpy as jnp
import numpy as np
from jax import lax

LEV = 72
KLEV = 20
STEPS = 8
CLON = 8
CLAT = 128
S_DEV = 4096
OWNERS = 16
CAP = 1024
SOUNDINGS = 131072
NLON = 32
NLAT = 512
CCOL = 1024
N_LAT = 4


def touch_ends(array, stream_key, smallest, largest):
    place = [jax.random.randint(jax.random.fold_in(stream_key, axis), (), 0, length) for axis, length in enumerate(array.shape)]
    widest = array.shape.index(max(array.shape))
    next_to = place[:widest] + [(place[widest] + 1) % array.shape[widest]] + place[widest + 1:]
    return array.at[tuple(place)].set(smallest).at[tuple(next_to)].set(largest)


def block_levels(own_key, dims, shards, smallest, top_value):
    level = 1.0
    for position, blocks in shards:
        steps = jax.random.uniform(jax.random.fold_in(jax.random.fold_in(own_key, 6), position), (blocks,), jnp.float32, smallest / len(shards), top_value / len(shards))
        level = level * jnp.repeat(jnp.exp(steps), dims[position] // blocks).reshape((-1,) + (1,) * (len(dims) - 1 - position))
    return level


def assign_block(key, own, number, rows, count, top, bound, slope):
    order = jax.random.permutation(key, count)
    heavy_load, ordinary = shares(count, rows * top, bound, slope, True), shares(count, rows * top, bound, slope, False)
    places = jnp.arange(count)

    def named(sizes, turn):
        used = int((sizes > 0).sum())
        fixed = max(1, used // 4)
        moved = fixed + (places - fixed + turn * (used - fixed)) % max(1, count - fixed)
        return jnp.zeros((count,), jnp.int32).at[order[jnp.where(places < fixed, places, moved)]].set(jnp.asarray(sizes, jnp.int32))

    sizes = jnp.where(number % 4 == 0, named(heavy_load, number // 4), named(ordinary, number - number // 4 - 1))
    mixed = jax.random.permutation(jax.random.fold_in(own, 3), count)
    source_of, taker = mixed[0:count // 2 * 2:2], mixed[1:count // 2 * 2:2]
    margin = jnp.minimum(sizes[source_of] - 1, bound - sizes[taker]) // 2
    margin = jnp.where((source_of == order[0]) | (taker == order[0]) | (sizes[taker] == 0), 0, jnp.maximum(margin, 0))
    moved = jax.random.randint(jax.random.fold_in(own, 4), (count // 2,), 0, 1 << 20) % (margin + 1)
    sizes = sizes.at[source_of].add(-moved).at[taker].add(moved)
    members = jnp.searchsorted(jnp.cumsum(sizes), jnp.arange(rows * top), side="right").astype(jnp.int32)
    grid = members.reshape(top, rows).T
    grid = grid[jax.random.permutation(jax.random.fold_in(own, 1), rows)]
    turn = jax.random.randint(jax.random.fold_in(own, 2), (rows, 1), 0, top)
    return jnp.take_along_axis(grid, (jnp.arange(top)[None, :] + turn) % top, axis=1)


def shares(amount, total, reach, skew, full):
    portions = [(1 << 20) // math.isqrt(rank ** skew) + 1 for rank in range(1, amount + 1)]
    largest = reach if full else min(reach, max(-(-total // amount), total * portions[0] // sum(portions)))
    least = 1 if total - largest >= amount - 1 else 0
    counts, spare = [largest] + [least] * (amount - 1), total - largest - least * (amount - 1)
    while spare > 0:
        free = [i for i in range(1, amount) if counts[i] < largest] or [i for i in range(1, amount) if counts[i] < reach]
        mass, budget = sum([portions[i] for i in free]), spare
        for i in free:
            addition = min(reach - counts[i], max(1, budget * portions[i] // mass), spare)
            counts[i] = counts[i] + addition
            spare = spare - addition
    return np.array(counts)


def centred(key, shape, width, limit, pieces=(), kind=jnp.bfloat16):
    array = jax.random.normal(key, shape, jnp.float32) * width
    if len(pieces) > 0:
        array = block_levels(key, shape, pieces, -0.22, 0.18) * array
    return jnp.clip(array, min=-limit, max=limit).astype(kind)


def setup_inputs(seed: int = 0) -> dict:
    streams_of = jax.random.split(jax.random.key(seed), 8)
    kernel = jnp.clip(0.2 + 1 * jax.random.uniform(streams_of[0], (KLEV, SOUNDINGS), jnp.float32) ** block_levels(streams_of[0], (KLEV, SOUNDINGS), ((1, 32),), -0.2, 0.2), 0.2, 1.2)
    residual = centred(streams_of[1], (SOUNDINGS,), 1.0, 6.0, ((0, 32),), jnp.float32)
    owner_block_keys = jax.random.split(jax.random.fold_in(streams_of[2], 1), SOUNDINGS // S_DEV)
    owner_block_turns = jax.random.permutation(jax.random.fold_in(streams_of[2], 3), SOUNDINGS // S_DEV)
    owner_block = jax.vmap(lambda own, number: assign_block(jax.random.fold_in(streams_of[2], 2), own, number, S_DEV, OWNERS, 1, CAP, 2))(owner_block_keys, owner_block_turns).reshape((SOUNDINGS, 1))
    column = touch_ends(jax.random.randint(streams_of[3], (SOUNDINGS,), 0, CCOL), jax.random.fold_in(streams_of[3], 1), 0, CCOL - 1).astype(jnp.int32)
    time_step = touch_ends(jax.random.randint(streams_of[4], (SOUNDINGS,), 0, STEPS), jax.random.fold_in(streams_of[4], 1), 0, STEPS - 1).astype(jnp.int32)
    horizontal = jnp.clip(0.04 + 0.18 * jax.random.uniform(streams_of[5], (4, LEV, NLON, NLAT), jnp.float32) ** block_levels(streams_of[5], (4, LEV, NLON, NLAT), ((2, 4), (3, 4)), -0.2, 0.2), 0.04, 0.22)
    vertical = jnp.clip(0.02 + 0.22 * jax.random.uniform(streams_of[6], (LEV - 1, NLON, NLAT), jnp.float32) ** block_levels(streams_of[6], (LEV - 1, NLON, NLAT), ((1, 4), (2, 4)), -0.2, 0.2), 0.02, 0.24)
    return {"kernel": kernel, "residual": residual, "owner_block": owner_block, "column": column, "time_step": time_step, "horizontal": horizontal, "vertical": vertical}


def level_map(levels, kernel_levels):
    heights = jnp.arange(levels, dtype=jnp.float32)
    centre = jnp.clip((heights + 0.5) * kernel_levels / levels - 0.5, 0.0, kernel_levels - 1.0)
    knots = jnp.arange(kernel_levels, dtype=jnp.float32)
    return jnp.maximum(0.0, 1.0 - jnp.abs(centre[:, None] - knots[None, :]))


def reference(kernel, residual, owner_block, column, time_step, horizontal, vertical):
    columns = NLON * NLAT
    owner_ids = owner_block[:, 0]
    longitude = (owner_ids // N_LAT) * CLON + column // CLAT
    latitude = (owner_ids % N_LAT) * CLAT + column % CLAT
    segment = (time_step * columns + longitude * NLAT + latitude).astype(jnp.int32)
    weighted = kernel * residual[None, :]
    binned = jnp.zeros((KLEV, STEPS * columns), jnp.float32).at[:, segment].add(weighted)
    binned = binned.reshape(KLEV, STEPS, columns)
    interp = level_map(LEV, KLEV)
    diagonal_part = 1.0 - horizontal[0] - horizontal[1] - horizontal[2] - horizontal[3]
    adjoint = jnp.zeros((LEV, NLON, NLAT), jnp.float32)
    flux_total = jnp.zeros((NLON, NLAT), jnp.float32)
    for step_index in range(STEPS - 1, -1, -1):
        forcing = jnp.dot(interp, binned[:, step_index, :], precision=lax.Precision.HIGHEST)
        forced = adjoint + forcing.reshape(LEV, NLON, NLAT)
        up_flux = vertical * (forced[1:] - forced[:-1])
        mixed = forced + jnp.pad(up_flux, ((0, 1), (0, 0), (0, 0))) - jnp.pad(up_flux, ((1, 0), (0, 0), (0, 0)))
        terms = horizontal * mixed[None]
        east_term = jnp.roll(terms[0], 1, axis=1)
        west_term = jnp.roll(terms[1], -1, axis=1)
        north_term = jnp.pad(terms[2][:, :, :-1], ((0, 0), (0, 0), (1, 0)))
        south_term = jnp.pad(terms[3][:, :, 1:], ((0, 0), (0, 0), (0, 1)))
        adjoint = diagonal_part * mixed + east_term + west_term + north_term + south_term
        flux_total = flux_total + adjoint[0]
    return adjoint, flux_total
```

```python
import functools

import jax
import jax.numpy as jnp
import numpy as np
from jax import lax
from jax.experimental import pallas as pl
from jax.experimental.pallas import tpu as pltpu
from jax.sharding import PartitionSpec as P

STEPS = 8
CLON = 8
CLAT = 128
CELLS = CLON * CLAT
ROWS = 24
CHUNK = 256
F32 = jnp.float32
BF16 = jnp.bfloat16
VMEM_LIMIT = 48 * 1024 * 1024
NT = (((1,), (1,)), ((), ()))


def level_weights(levels, kernel_levels):
    one = np.float32
    heights = np.arange(levels, dtype=np.float32)
    centre = np.clip((heights + one(0.5)) * one(kernel_levels) / one(levels) - one(0.5),
                     one(0), one(kernel_levels - 1))
    knots = np.arange(kernel_levels, dtype=np.float32)
    return np.maximum(one(0), one(1) - np.abs(centre[:, None] - knots[None, :]))


def split(values):
    high = values.astype(BF16)
    return high, (values - high.astype(F32)).astype(BF16)


def pack_kernel(owners, capacity, starts_ref, kernel_ref, residual_ref, owner_ref, segment_ref,
                out_ref, data_ref, place_ref, sorted_ref):
    levels, count = kernel_ref.shape
    chunks = count // CHUNK
    half = data_ref.shape[0] // 2
    high, low = split(kernel_ref[...] * residual_ref[...])
    segment = segment_ref[...]
    spare = jnp.zeros((half - levels - 1, count), F32)
    seg_high = (segment // CLAT * CLAT).astype(F32)
    seg_low = (segment % CLAT).astype(F32)
    data_ref[0:half] = jnp.concatenate(
        [high.astype(F32), seg_high, spare], axis=0).astype(BF16)
    data_ref[half:] = jnp.concatenate(
        [low.astype(F32), seg_low, spare], axis=0).astype(BF16)

    names = lax.broadcasted_iota(jnp.int32, (owners, CHUNK), 0)
    earlier = (lax.broadcasted_iota(jnp.int32, (CHUNK, CHUNK), 0)
               < lax.broadcasted_iota(jnp.int32, (CHUNK, CHUNK), 1)).astype(F32).astype(BF16)
    totals = jnp.zeros((owners, 1), F32)
    for c in range(chunks):
        own = (owner_ref[:, c * CHUNK:(c + 1) * CHUNK] == names).astype(F32)
        totals = totals + jnp.sum(own, axis=1, keepdims=True)
    before = (lax.broadcasted_iota(jnp.int32, (owners, owners), 1)
              < lax.broadcasted_iota(jnp.int32, (owners, owners), 0)).astype(F32)
    carry = jnp.dot(before, jnp.broadcast_to(totals, (owners, CHUNK)),
                    precision=lax.Precision.HIGHEST, preferred_element_type=F32)[:, 0:1]
    for c in range(chunks):
        own = (owner_ref[:, c * CHUNK:(c + 1) * CHUNK] == names).astype(F32)
        inside = jnp.dot(own.astype(BF16), earlier, preferred_element_type=F32)
        place_ref[:, c * CHUNK:(c + 1) * CHUNK] = jnp.sum(
            own * (inside + carry), axis=0, keepdims=True).astype(jnp.int32)
        carry = carry + jnp.sum(own, axis=1, keepdims=True)

    def arrange(block, _):
        base = block * CHUNK
        target = lax.broadcasted_iota(jnp.int32, (CHUNK, count), 0) + base
        chosen = (target == place_ref[...]).astype(F32).astype(BF16)
        got = lax.dot_general(data_ref[...], chosen, NT, preferred_element_type=F32)
        sorted_ref[:, pl.ds(pl.multiple_of(base, CHUNK), CHUNK)] = got[0:ROWS] + got[half:half + ROWS]
        return 0

    lax.fori_loop(0, chunks, arrange, 0)
    sorted_ref[:, count:] = jnp.zeros((ROWS, sorted_ref.shape[1] - count), F32)
    window = capacity + CLAT
    slot = lax.broadcasted_iota(jnp.int32, (ROWS, capacity), 1)
    row = lax.broadcasted_iota(jnp.int32, (ROWS, capacity), 0)

    def hand_out(name, _):
        start = starts_ref[name]
        length = starts_ref[name + 1] - start
        aligned = start // CLAT * CLAT
        run = sorted_ref[:, pl.ds(pl.multiple_of(aligned, CLAT), window)]
        run = pltpu.roll(run, lax.rem(window - (start - aligned), window), 1)[:, 0:capacity]
        out_ref[name] = jnp.where((row == levels) & (slot >= length), -1.0, run)
        return 0

    lax.fori_loop(0, owners, hand_out, 0)


def pack(kernel, residual, owner_block, column, time_step, owners, capacity):
    levels, count = kernel.shape
    owner = owner_block.reshape(1, count)
    segment = (time_step * CELLS + column).reshape(1, count)
    labels = jnp.arange(owners + 1, dtype=jnp.int32)
    starts = jnp.sum((owner < labels[:, None]).astype(jnp.int32), axis=1)
    vmem = pl.BlockSpec(memory_space=pltpu.VMEM)
    return pl.pallas_call(
        functools.partial(pack_kernel, owners, capacity),
        out_shape=jax.ShapeDtypeStruct((owners, ROWS, capacity), F32),
        in_specs=[pl.BlockSpec(memory_space=pltpu.SMEM)] + [vmem] * 4,
        out_specs=vmem,
        scratch_shapes=[
            pltpu.VMEM((64, count), BF16),
            pltpu.VMEM((1, count), jnp.int32),
            pltpu.VMEM((ROWS, count + capacity + CLAT), F32),
        ],
        compiler_params=pltpu.CompilerParams(vmem_limit_bytes=VMEM_LIMIT),
    )(starts, kernel, residual.reshape(1, count), owner, segment)


def bin_kernel(levels, got_ref, out_ref, total_ref):
    source = pl.program_id(0)
    capacity = got_ref.shape[2]
    width = min(capacity, CHUNK)
    half = STEPS * ROWS

    @pl.when(source == 0)
    def _():
        total_ref[...] = jnp.zeros_like(total_ref)

    for piece in range(capacity // width):
        rows = got_ref[0, :, piece * width:(piece + 1) * width]
        segment = rows[levels:levels + 1].astype(jnp.int32)

        @pl.when(jnp.max(rows[levels:levels + 1]) >= 0.0)
        def _():
            step = jnp.broadcast_to(segment >> 10, (ROWS, width))
            cell = segment & (CELLS - 1)
            place = lax.broadcasted_iota(jnp.int32, (CELLS, width), 0)
            chosen = (place == cell).astype(F32).astype(BF16)
            taken = jnp.concatenate(
                [jnp.where(step == j, rows, 0.0) for j in range(STEPS)], axis=0)
            high = taken.astype(BF16)
            low = (taken - high.astype(F32)).astype(BF16)
            total_ref[...] += lax.dot_general(
                jnp.concatenate([high, low], axis=0), chosen, NT, preferred_element_type=F32)

    @pl.when(source == pl.num_programs(0) - 1)
    def _():
        for i in range(CLON):
            part = (total_ref[0:half, i * CLAT:(i + 1) * CLAT]
                    + total_ref[half:, i * CLAT:(i + 1) * CLAT])
            for j in range(STEPS):
                out_ref[j, :, i, :] = part[j * ROWS:j * ROWS + levels]


def bin_soundings(got, levels):
    owners, rows, capacity = got.shape
    return pl.pallas_call(
        functools.partial(bin_kernel, levels),
        out_shape=jax.ShapeDtypeStruct((STEPS, levels, CLON, CLAT), F32),
        grid=(owners,),
        in_specs=[pl.BlockSpec((1, rows, capacity), lambda i: (i, 0, 0))],
        out_specs=pl.BlockSpec((STEPS, levels, CLON, CLAT), lambda i: (0, 0, 0, 0)),
        scratch_shapes=[pltpu.VMEM((2 * STEPS * ROWS, CELLS), F32)],
        compiler_params=pltpu.CompilerParams(vmem_limit_bytes=VMEM_LIMIT),
    )(got)


def steps_kernel(orbits, lons, lats, weights, bins_ref, horizontal_ref, vertical_ref,
                 adjoint_ref, flux_ref, other_ref, term_ref, diagonal_ref,
                 lon_out, lon_in, lat_out, lat_in,
                 orbit_send, orbit_recv, edge_send, edge_recv):
    levels = adjoint_ref.shape[0]
    lon, lat, orbit = lax.axis_index("lon"), lax.axis_index("lat"), lax.axis_index("orbit")
    east, west = lax.rem(lon + 1, lons), lax.rem(lon + lons - 1, lons)
    partner = 1 - orbit
    mesh_id = pl.DeviceIdType.MESH
    barrier = pltpu.get_barrier_semaphore()
    pl.semaphore_signal(barrier, inc=1, device_id={"lon": east}, device_id_type=mesh_id)
    pl.semaphore_signal(barrier, inc=1, device_id={"lon": west}, device_id_type=mesh_id)
    pl.semaphore_signal(barrier, inc=1, device_id={"orbit": partner}, device_id_type=mesh_id)

    @pl.when(lat < lats - 1)
    def _():
        pl.semaphore_signal(barrier, inc=1, device_id={"lat": lat + 1}, device_id_type=mesh_id)

    @pl.when(lat > 0)
    def _():
        pl.semaphore_signal(barrier, inc=1, device_id={"lat": lat - 1}, device_id_type=mesh_id)

    peers = 3 + jnp.where(lat > 0, 1, 0) + jnp.where(lat < lats - 1, 1, 0)
    pl.semaphore_wait(barrier, peers)

    def orbit_copy(j):
        return pltpu.make_async_remote_copy(
            src_ref=bins_ref.at[j], dst_ref=other_ref.at[j],
            send_sem=orbit_send.at[j], recv_sem=orbit_recv.at[j],
            device_id={"orbit": partner}, device_id_type=mesh_id)

    def edge_copy(t, side):
        out, into = (lon_out, lon_in) if side < 2 else (lat_out, lat_in)
        device = ({"lon": east}, {"lon": west}, {"lat": lat + 1}, {"lat": lat - 1})[side]
        return pltpu.make_async_remote_copy(
            src_ref=out.at[side % 2, t], dst_ref=into.at[side % 2, t],
            send_sem=edge_send.at[side, t], recv_sem=edge_recv.at[side, t],
            device_id=device, device_id_type=mesh_id)

    def begin(t, _):
        orbit_copy(STEPS - 1 - t).start()
        return 0

    lax.fori_loop(0, STEPS, begin, 0)

    @pl.when(lat == 0)
    def _():
        lat_in[0] = jnp.zeros(lat_in.shape[1:], F32)

    @pl.when(lat == lats - 1)
    def _():
        lat_in[1] = jnp.zeros(lat_in.shape[1:], F32)

    diagonal_ref[...] = (1.0 - horizontal_ref[0] - horizontal_ref[1]
                         - horizontal_ref[2] - horizontal_ref[3])
    adjoint_ref[...] = jnp.zeros_like(adjoint_ref)
    flux_ref[...] = jnp.zeros_like(flux_ref)
    shape = adjoint_ref.shape
    lane = lax.broadcasted_iota(jnp.int32, shape, 2)
    sub = lax.broadcasted_iota(jnp.int32, shape, 1)
    level = lax.broadcasted_iota(jnp.int32, shape, 0)

    def advance(t, _):
        j = STEPS - 1 - t
        orbit_copy(j).wait_recv()
        bins = bins_ref[j] + other_ref[j]
        forcing = []
        for l in range(levels):
            parts = [bins[k:k + 1] * float(weights[l, k]) for k in np.nonzero(weights[l])[0]]
            forcing.append(functools.reduce(lambda a, b: a + b, parts))
        forced = adjoint_ref[...] + jnp.concatenate(forcing, axis=0)
        up = vertical_ref[...] * (forced[1:] - forced[:-1])
        none = jnp.zeros((1, CLON, CLAT), F32)
        mixed = (forced + jnp.concatenate([up, none], axis=0)
                 - jnp.concatenate([none, up], axis=0))
        term_ref[0] = horizontal_ref[0] * mixed
        term_ref[1] = horizontal_ref[1] * mixed
        north = horizontal_ref[2] * mixed
        south = horizontal_ref[3] * mixed
        lon_out[0, t] = term_ref[0, :, CLON - 1, :]
        lon_out[1, t] = term_ref[1, :, 0, :]
        edge_copy(t, 0).start()
        edge_copy(t, 1).start()
        lat_out[0, t] = jnp.sum(jnp.where(
            lane == level, jnp.broadcast_to(north[:, :, CLAT - 1:CLAT], shape), 0.0), axis=0)
        lat_out[1, t] = jnp.sum(jnp.where(
            lane == level, jnp.broadcast_to(south[:, :, 0:1], shape), 0.0), axis=0)

        @pl.when(lat < lats - 1)
        def _():
            edge_copy(t, 2).start()

        @pl.when(lat > 0)
        def _():
            edge_copy(t, 3).start()

        inside = (diagonal_ref[...] * mixed
                  + jnp.where(sub == 0, 0.0, pltpu.roll(term_ref[0], 1, 1))
                  + jnp.where(sub == CLON - 1, 0.0, pltpu.roll(term_ref[1], CLON - 1, 1))
                  + jnp.where(lane == 0, 0.0, pltpu.roll(north, 1, 2))
                  + jnp.where(lane == CLAT - 1, 0.0, pltpu.roll(south, CLAT - 1, 2)))
        adjoint_ref[...] = inside

        @pl.when(lat > 0)
        def _():
            edge_copy(t, 2).wait_recv()

        @pl.when(lat < lats - 1)
        def _():
            edge_copy(t, 3).wait_recv()

        edge_copy(t, 0).wait_recv()
        edge_copy(t, 1).wait_recv()
        low = jnp.sum(jnp.where(lane == level, lat_in[0, t][None], 0.0), axis=2, keepdims=True)
        high = jnp.sum(jnp.where(lane == level, lat_in[1, t][None], 0.0), axis=2, keepdims=True)
        first = lon_in[0, t].reshape(levels, 1, CLAT)
        last = lon_in[1, t].reshape(levels, 1, CLAT)
        result = (adjoint_ref[...]
                  + jnp.where(sub == 0, first, 0.0) + jnp.where(sub == CLON - 1, last, 0.0)
                  + jnp.where(lane == 0, low, 0.0) + jnp.where(lane == CLAT - 1, high, 0.0))
        adjoint_ref[...] = result
        flux_ref[...] += result[0]
        return 0

    lax.fori_loop(0, STEPS, advance, 0)

    def finish(t, _):
        orbit_copy(t).wait_send()
        edge_copy(t, 0).wait_send()
        edge_copy(t, 1).wait_send()

        @pl.when(lat < lats - 1)
        def _():
            edge_copy(t, 2).wait_send()

        @pl.when(lat > 0)
        def _():
            edge_copy(t, 3).wait_send()

        return 0

    lax.fori_loop(0, STEPS, finish, 0)


def transport(bins, horizontal, vertical):
    levels = horizontal.shape[1]
    kernel_levels = bins.shape[1]
    orbits, lons, lats = (lax.axis_size(name) for name in ("orbit", "lon", "lat"))
    vmem = pl.BlockSpec(memory_space=pltpu.VMEM)
    block = (levels, CLON, CLAT)
    return pl.pallas_call(
        functools.partial(steps_kernel, orbits, lons, lats, level_weights(levels, kernel_levels)),
        out_shape=(jax.ShapeDtypeStruct(block, F32), jax.ShapeDtypeStruct((CLON, CLAT), F32)),
        in_specs=[vmem] * 3,
        out_specs=(vmem, vmem),
        scratch_shapes=[
            pltpu.VMEM(bins.shape, F32),
            pltpu.VMEM((2,) + block, F32),
            pltpu.VMEM(block, F32),
            pltpu.VMEM((2, STEPS, levels, CLAT), F32),
            pltpu.VMEM((2, STEPS, levels, CLAT), F32),
            pltpu.VMEM((2, STEPS, CLON, CLAT), F32),
            pltpu.VMEM((2, STEPS, CLON, CLAT), F32),
            pltpu.SemaphoreType.DMA((STEPS,)),
            pltpu.SemaphoreType.DMA((STEPS,)),
            pltpu.SemaphoreType.DMA((4, STEPS)),
            pltpu.SemaphoreType.DMA((4, STEPS)),
        ],
        compiler_params=pltpu.CompilerParams(
            collective_id=0, has_side_effects=True, vmem_limit_bytes=VMEM_LIMIT),
    )(bins, horizontal, vertical)


def per_device(kernel, residual, owner_block, column, time_step, horizontal, vertical):
    owners = lax.axis_size("lon") * lax.axis_size("lat")
    capacity = 4 * kernel.shape[1] // owners
    slots = pack(kernel, residual, owner_block, column, time_step, owners, capacity)
    got = lax.all_to_all(slots, ("lon", "lat"), split_axis=0, concat_axis=0, tiled=True)
    return transport(bin_soundings(got, kernel.shape[0]), horizontal, vertical)


def solution(mesh):
    placed = (
        P(None, ("orbit", "lon", "lat")),
        P(("orbit", "lon", "lat")),
        P(("orbit", "lon", "lat"), None),
        P(("orbit", "lon", "lat")),
        P(("orbit", "lon", "lat")),
        P(None, None, "lon", "lat"),
        P(None, "lon", "lat"),
    )
    return jax.shard_map(
        per_device,
        mesh=mesh,
        in_specs=placed,
        out_specs=(P(None, "lon", "lat"), P("lon", "lat")),
        check_vma=False,
    )
```

```python
import functools

import jax
import jax.numpy as jnp
import numpy as np
from jax import lax
from jax.experimental import pallas as pl
from jax.experimental.pallas import tpu as pltpu
from jax.sharding import PartitionSpec as P

STEPS = 8
CLON = 8
CLAT = 128
CELLS = CLON * CLAT
ROWS = 24
CHUNK = 256
F32 = jnp.float32
BF16 = jnp.bfloat16
VMEM_LIMIT = 48 * 1024 * 1024
NT = (((1,), (1,)), ((), ()))


def level_weights(levels, kernel_levels):
    one = np.float32
    heights = np.arange(levels, dtype=np.float32)
    centre = np.clip((heights + one(0.5)) * one(kernel_levels) / one(levels) - one(0.5),
                     one(0), one(kernel_levels - 1))
    knots = np.arange(kernel_levels, dtype=np.float32)
    return np.maximum(one(0), one(1) - np.abs(centre[:, None] - knots[None, :]))


def split(values):
    high = values.astype(BF16)
    return high, (values - high.astype(F32)).astype(BF16)


def pack_kernel(owners, capacity, starts_ref, kernel_ref, residual_ref, owner_ref, segment_ref,
                out_ref, data_ref, place_ref, sorted_ref):
    levels, count = kernel_ref.shape
    chunks = count // CHUNK
    half = data_ref.shape[0] // 2
    high, low = split(kernel_ref[...] * residual_ref[...])
    segment = segment_ref[...]
    spare = jnp.zeros((half - levels - 1, count), F32)
    seg_high = (segment // CLAT * CLAT).astype(F32)
    seg_low = (segment % CLAT).astype(F32)
    data_ref[0:half] = jnp.concatenate(
        [high.astype(F32), seg_high, spare], axis=0).astype(BF16)
    data_ref[half:] = jnp.concatenate(
        [low.astype(F32), seg_low, spare], axis=0).astype(BF16)

    names = lax.broadcasted_iota(jnp.int32, (owners, CHUNK), 0)
    earlier = (lax.broadcasted_iota(jnp.int32, (CHUNK, CHUNK), 0)
               < lax.broadcasted_iota(jnp.int32, (CHUNK, CHUNK), 1)).astype(F32).astype(BF16)
    totals = jnp.zeros((owners, 1), F32)
    for c in range(chunks):
        own = (owner_ref[:, c * CHUNK:(c + 1) * CHUNK] == names).astype(F32)
        totals = totals + jnp.sum(own, axis=1, keepdims=True)
    before = (lax.broadcasted_iota(jnp.int32, (owners, owners), 1)
              < lax.broadcasted_iota(jnp.int32, (owners, owners), 0)).astype(F32)
    carry = jnp.dot(before, jnp.broadcast_to(totals, (owners, CHUNK)),
                    precision=lax.Precision.HIGHEST, preferred_element_type=F32)[:, 0:1]
    for c in range(chunks):
        own = (owner_ref[:, c * CHUNK:(c + 1) * CHUNK] == names).astype(F32)
        inside = jnp.dot(own.astype(BF16), earlier, preferred_element_type=F32)
        place_ref[:, c * CHUNK:(c + 1) * CHUNK] = jnp.sum(
            own * (inside + carry), axis=0, keepdims=True).astype(jnp.int32)
        carry = carry + jnp.sum(own, axis=1, keepdims=True)

    def arrange(block, _):
        base = block * CHUNK
        target = lax.broadcasted_iota(jnp.int32, (CHUNK, count), 0) + base
        chosen = (target == place_ref[...]).astype(F32).astype(BF16)
        got = lax.dot_general(data_ref[...], chosen, NT, preferred_element_type=F32)
        sorted_ref[:, pl.ds(pl.multiple_of(base, CHUNK), CHUNK)] = got[0:ROWS] + got[half:half + ROWS]
        return 0

    lax.fori_loop(0, chunks, arrange, 0)
    sorted_ref[:, count:] = jnp.zeros((ROWS, sorted_ref.shape[1] - count), F32)
    window = capacity + CLAT
    slot = lax.broadcasted_iota(jnp.int32, (ROWS, capacity), 1)
    row = lax.broadcasted_iota(jnp.int32, (ROWS, capacity), 0)

    def hand_out(name, _):
        start = starts_ref[name]
        length = starts_ref[name + 1] - start
        aligned = start // CLAT * CLAT
        run = sorted_ref[:, pl.ds(pl.multiple_of(aligned, CLAT), window)]
        run = pltpu.roll(run, lax.rem(window - (start - aligned), window), 1)[:, 0:capacity]
        out_ref[name] = jnp.where((row == levels) & (slot >= length), -1.0, run)[0:levels + 1]
        return 0

    lax.fori_loop(0, owners, hand_out, 0)


def pack(kernel, residual, owner_block, column, time_step, owners, capacity):
    levels, count = kernel.shape
    owner = owner_block.reshape(1, count)
    segment = (time_step * CELLS + column).reshape(1, count)
    labels = jnp.arange(owners + 1, dtype=jnp.int32)
    starts = jnp.sum((owner < labels[:, None]).astype(jnp.int32), axis=1)
    vmem = pl.BlockSpec(memory_space=pltpu.VMEM)
    return pl.pallas_call(
        functools.partial(pack_kernel, owners, capacity),
        out_shape=jax.ShapeDtypeStruct((owners, levels + 1, capacity), F32),
        in_specs=[pl.BlockSpec(memory_space=pltpu.SMEM)] + [vmem] * 4,
        out_specs=vmem,
        scratch_shapes=[
            pltpu.VMEM((64, count), BF16),
            pltpu.VMEM((1, count), jnp.int32),
            pltpu.VMEM((ROWS, count + capacity + CLAT), F32),
        ],
        compiler_params=pltpu.CompilerParams(vmem_limit_bytes=VMEM_LIMIT),
    )(starts, kernel, residual.reshape(1, count), owner, segment)


def bin_kernel(levels, lons, lats, slots_ref, out_ref, got_ref, total_ref, send_sem, recv_sem):
    owners, _, capacity = slots_ref.shape
    lon, lat = lax.axis_index("lon"), lax.axis_index("lat")
    mesh_id = pl.DeviceIdType.MESH
    half = STEPS * ROWS
    width = min(capacity, 2 * CHUNK)

    def peer(d):
        return lax.rem(lon + d // lats, lons), lax.rem(lat + lax.rem(d, lats), lats)

    def slot_copy(d):
        to_lon, to_lat = peer(d)
        return pltpu.make_async_remote_copy(
            src_ref=slots_ref.at[to_lon * lats + to_lat], dst_ref=got_ref.at[d],
            send_sem=send_sem.at[d], recv_sem=recv_sem.at[d],
            device_id={"lon": to_lon, "lat": to_lat}, device_id_type=mesh_id)

    barrier = pltpu.get_barrier_semaphore()

    def greet(d, _):
        to_lon, to_lat = peer(d)
        pl.semaphore_signal(barrier, inc=1, device_id={"lon": to_lon, "lat": to_lat},
                            device_id_type=mesh_id)
        return 0

    lax.fori_loop(1, owners, greet, 0)
    pl.semaphore_wait(barrier, owners - 1)

    def begin(d, _):
        slot_copy(d).start()
        return 0

    lax.fori_loop(1, owners, begin, 0)
    total_ref[...] = jnp.zeros_like(total_ref)
    got_ref[0] = slots_ref[lon * lats + lat]

    def collect(d, _):
        @pl.when(d > 0)
        def _():
            slot_copy(d).wait_recv()

        for piece in range(capacity // width):
            rows = got_ref[d, :, piece * width:(piece + 1) * width]
            segment = rows[levels:levels + 1].astype(jnp.int32)
            values = jnp.concatenate(
                [rows[0:levels], jnp.zeros((ROWS - levels, width), F32)], axis=0)
            step = jnp.broadcast_to(segment >> 10, (ROWS, width))
            cell = segment & (CELLS - 1)
            place = lax.broadcasted_iota(jnp.int32, (CELLS, width), 0)
            chosen = (place == cell).astype(F32).astype(BF16)
            taken = jnp.concatenate(
                [jnp.where(step == j, values, 0.0) for j in range(STEPS)], axis=0)
            high = taken.astype(BF16)
            low = (taken - high.astype(F32)).astype(BF16)
            total_ref[...] += lax.dot_general(
                jnp.concatenate([high, low], axis=0), chosen, NT, preferred_element_type=F32)
        return 0

    lax.fori_loop(0, owners, collect, 0)
    for i in range(CLON):
        part = (total_ref[0:half, i * CLAT:(i + 1) * CLAT]
                + total_ref[half:, i * CLAT:(i + 1) * CLAT])
        for j in range(STEPS):
            out_ref[j, :, i, :] = part[j * ROWS:j * ROWS + levels]

    def finish(d, _):
        slot_copy(d).wait_send()
        return 0

    lax.fori_loop(1, owners, finish, 0)


def bin_soundings(slots, levels):
    lons, lats = lax.axis_size("lon"), lax.axis_size("lat")
    vmem = pl.BlockSpec(memory_space=pltpu.VMEM)
    return pl.pallas_call(
        functools.partial(bin_kernel, levels, lons, lats),
        out_shape=jax.ShapeDtypeStruct((STEPS, levels, CLON, CLAT), F32),
        in_specs=[vmem],
        out_specs=vmem,
        scratch_shapes=[
            pltpu.VMEM(slots.shape, F32),
            pltpu.VMEM((2 * STEPS * ROWS, CELLS), F32),
            pltpu.SemaphoreType.DMA((lons * lats,)),
            pltpu.SemaphoreType.DMA((lons * lats,)),
        ],
        compiler_params=pltpu.CompilerParams(
            collective_id=1, has_side_effects=True, vmem_limit_bytes=VMEM_LIMIT),
    )(slots)


def steps_kernel(orbits, lons, lats, weights, bins_ref, horizontal_ref, vertical_ref,
                 adjoint_ref, flux_ref, other_ref, term_ref, diagonal_ref,
                 lon_out, lon_in, lat_out, lat_in,
                 orbit_send, orbit_recv, edge_send, edge_recv):
    levels = adjoint_ref.shape[0]
    lon, lat, orbit = lax.axis_index("lon"), lax.axis_index("lat"), lax.axis_index("orbit")
    east, west = lax.rem(lon + 1, lons), lax.rem(lon + lons - 1, lons)
    partner = 1 - orbit
    mesh_id = pl.DeviceIdType.MESH
    barrier = pltpu.get_barrier_semaphore()
    pl.semaphore_signal(barrier, inc=1, device_id={"lon": east}, device_id_type=mesh_id)
    pl.semaphore_signal(barrier, inc=1, device_id={"lon": west}, device_id_type=mesh_id)
    pl.semaphore_signal(barrier, inc=1, device_id={"orbit": partner}, device_id_type=mesh_id)

    @pl.when(lat < lats - 1)
    def _():
        pl.semaphore_signal(barrier, inc=1, device_id={"lat": lat + 1}, device_id_type=mesh_id)

    @pl.when(lat > 0)
    def _():
        pl.semaphore_signal(barrier, inc=1, device_id={"lat": lat - 1}, device_id_type=mesh_id)

    peers = 3 + jnp.where(lat > 0, 1, 0) + jnp.where(lat < lats - 1, 1, 0)
    pl.semaphore_wait(barrier, peers)

    def orbit_copy(j):
        return pltpu.make_async_remote_copy(
            src_ref=bins_ref.at[j], dst_ref=other_ref.at[j],
            send_sem=orbit_send.at[j], recv_sem=orbit_recv.at[j],
            device_id={"orbit": partner}, device_id_type=mesh_id)

    def edge_copy(t, side):
        out, into = (lon_out, lon_in) if side < 2 else (lat_out, lat_in)
        device = ({"lon": east}, {"lon": west}, {"lat": lat + 1}, {"lat": lat - 1})[side]
        return pltpu.make_async_remote_copy(
            src_ref=out.at[side % 2, t], dst_ref=into.at[side % 2, t],
            send_sem=edge_send.at[side, t], recv_sem=edge_recv.at[side, t],
            device_id=device, device_id_type=mesh_id)

    def begin(t, _):
        orbit_copy(STEPS - 1 - t).start()
        return 0

    lax.fori_loop(0, STEPS, begin, 0)

    @pl.when(lat == 0)
    def _():
        lat_in[0] = jnp.zeros(lat_in.shape[1:], F32)

    @pl.when(lat == lats - 1)
    def _():
        lat_in[1] = jnp.zeros(lat_in.shape[1:], F32)

    diagonal_ref[...] = (1.0 - horizontal_ref[0] - horizontal_ref[1]
                         - horizontal_ref[2] - horizontal_ref[3])
    adjoint_ref[...] = jnp.zeros_like(adjoint_ref)
    flux_ref[...] = jnp.zeros_like(flux_ref)
    shape = adjoint_ref.shape
    lane = lax.broadcasted_iota(jnp.int32, shape, 2)
    sub = lax.broadcasted_iota(jnp.int32, shape, 1)
    level = lax.broadcasted_iota(jnp.int32, shape, 0)

    def advance(t, _):
        j = STEPS - 1 - t
        orbit_copy(j).wait_recv()
        bins = bins_ref[j] + other_ref[j]
        forcing = []
        for l in range(levels):
            parts = [bins[k:k + 1] * float(weights[l, k]) for k in np.nonzero(weights[l])[0]]
            forcing.append(functools.reduce(lambda a, b: a + b, parts))
        forced = adjoint_ref[...] + jnp.concatenate(forcing, axis=0)
        up = vertical_ref[...] * (forced[1:] - forced[:-1])
        none = jnp.zeros((1, CLON, CLAT), F32)
        mixed = (forced + jnp.concatenate([up, none], axis=0)
                 - jnp.concatenate([none, up], axis=0))
        term_ref[0] = horizontal_ref[0] * mixed
        term_ref[1] = horizontal_ref[1] * mixed
        north = horizontal_ref[2] * mixed
        south = horizontal_ref[3] * mixed
        lon_out[0, t] = term_ref[0, :, CLON - 1, :]
        lon_out[1, t] = term_ref[1, :, 0, :]
        edge_copy(t, 0).start()
        edge_copy(t, 1).start()
        lat_out[0, t] = jnp.sum(jnp.where(
            lane == level, jnp.broadcast_to(north[:, :, CLAT - 1:CLAT], shape), 0.0), axis=0)
        lat_out[1, t] = jnp.sum(jnp.where(
            lane == level, jnp.broadcast_to(south[:, :, 0:1], shape), 0.0), axis=0)

        @pl.when(lat < lats - 1)
        def _():
            edge_copy(t, 2).start()

        @pl.when(lat > 0)
        def _():
            edge_copy(t, 3).start()

        inside = (diagonal_ref[...] * mixed
                  + jnp.where(sub == 0, 0.0, pltpu.roll(term_ref[0], 1, 1))
                  + jnp.where(sub == CLON - 1, 0.0, pltpu.roll(term_ref[1], CLON - 1, 1))
                  + jnp.where(lane == 0, 0.0, pltpu.roll(north, 1, 2))
                  + jnp.where(lane == CLAT - 1, 0.0, pltpu.roll(south, CLAT - 1, 2)))
        adjoint_ref[...] = inside

        @pl.when(lat > 0)
        def _():
            edge_copy(t, 2).wait_recv()

        @pl.when(lat < lats - 1)
        def _():
            edge_copy(t, 3).wait_recv()

        edge_copy(t, 0).wait_recv()
        edge_copy(t, 1).wait_recv()
        low = jnp.sum(jnp.where(lane == level, lat_in[0, t][None], 0.0), axis=2, keepdims=True)
        high = jnp.sum(jnp.where(lane == level, lat_in[1, t][None], 0.0), axis=2, keepdims=True)
        first = lon_in[0, t].reshape(levels, 1, CLAT)
        last = lon_in[1, t].reshape(levels, 1, CLAT)
        result = (adjoint_ref[...]
                  + jnp.where(sub == 0, first, 0.0) + jnp.where(sub == CLON - 1, last, 0.0)
                  + jnp.where(lane == 0, low, 0.0) + jnp.where(lane == CLAT - 1, high, 0.0))
        adjoint_ref[...] = result
        flux_ref[...] += result[0]
        return 0

    lax.fori_loop(0, STEPS, advance, 0)

    def finish(t, _):
        orbit_copy(t).wait_send()
        edge_copy(t, 0).wait_send()
        edge_copy(t, 1).wait_send()

        @pl.when(lat < lats - 1)
        def _():
            edge_copy(t, 2).wait_send()

        @pl.when(lat > 0)
        def _():
            edge_copy(t, 3).wait_send()

        return 0

    lax.fori_loop(0, STEPS, finish, 0)


def transport(bins, horizontal, vertical):
    levels = horizontal.shape[1]
    kernel_levels = bins.shape[1]
    orbits, lons, lats = (lax.axis_size(name) for name in ("orbit", "lon", "lat"))
    vmem = pl.BlockSpec(memory_space=pltpu.VMEM)
    block = (levels, CLON, CLAT)
    return pl.pallas_call(
        functools.partial(steps_kernel, orbits, lons, lats, level_weights(levels, kernel_levels)),
        out_shape=(jax.ShapeDtypeStruct(block, F32), jax.ShapeDtypeStruct((CLON, CLAT), F32)),
        in_specs=[vmem] * 3,
        out_specs=(vmem, vmem),
        scratch_shapes=[
            pltpu.VMEM(bins.shape, F32),
            pltpu.VMEM((2,) + block, F32),
            pltpu.VMEM(block, F32),
            pltpu.VMEM((2, STEPS, levels, CLAT), F32),
            pltpu.VMEM((2, STEPS, levels, CLAT), F32),
            pltpu.VMEM((2, STEPS, CLON, CLAT), F32),
            pltpu.VMEM((2, STEPS, CLON, CLAT), F32),
            pltpu.SemaphoreType.DMA((STEPS,)),
            pltpu.SemaphoreType.DMA((STEPS,)),
            pltpu.SemaphoreType.DMA((4, STEPS)),
            pltpu.SemaphoreType.DMA((4, STEPS)),
        ],
        compiler_params=pltpu.CompilerParams(
            collective_id=0, has_side_effects=True, vmem_limit_bytes=VMEM_LIMIT),
    )(bins, horizontal, vertical)


def per_device(kernel, residual, owner_block, column, time_step, horizontal, vertical):
    owners = lax.axis_size("lon") * lax.axis_size("lat")
    capacity = 4 * kernel.shape[1] // owners
    slots = pack(kernel, residual, owner_block, column, time_step, owners, capacity)
    return transport(bin_soundings(slots, kernel.shape[0]), horizontal, vertical)


def solution(mesh):
    placed = (
        P(None, ("orbit", "lon", "lat")),
        P(("orbit", "lon", "lat")),
        P(("orbit", "lon", "lat"), None),
        P(("orbit", "lon", "lat")),
        P(("orbit", "lon", "lat")),
        P(None, None, "lon", "lat"),
        P(None, "lon", "lat"),
    )
    return jax.shard_map(
        per_device,
        mesh=mesh,
        in_specs=placed,
        out_specs=(P(None, "lon", "lat"), P("lon", "lat")),
        check_vma=False,
    )
```

```python
import functools

import jax
import jax.numpy as jnp
import numpy as np
from jax import lax
from jax.experimental import pallas as pl
from jax.experimental.pallas import tpu as pltpu
from jax.sharding import PartitionSpec as P

STEPS = 8
CLON = 8
CLAT = 128
CELLS = CLON * CLAT
ROWS = 24
CHUNK = 256
F32 = jnp.float32
BF16 = jnp.bfloat16
VMEM_LIMIT = 48 * 1024 * 1024
NT = (((1,), (1,)), ((), ()))


def level_weights(levels, kernel_levels):
    one = np.float32
    heights = np.arange(levels, dtype=np.float32)
    centre = np.clip((heights + one(0.5)) * one(kernel_levels) / one(levels) - one(0.5),
                     one(0), one(kernel_levels - 1))
    knots = np.arange(kernel_levels, dtype=np.float32)
    return np.maximum(one(0), one(1) - np.abs(centre[:, None] - knots[None, :]))


def split(values):
    high = values.astype(BF16)
    return high, (values - high.astype(F32)).astype(BF16)


def pack_kernel(owners, capacity, starts_ref, kernel_ref, residual_ref, owner_ref, segment_ref,
                out_ref, data_ref, place_ref, sorted_ref):
    levels, count = kernel_ref.shape
    chunks = count // CHUNK
    half = data_ref.shape[0] // 2
    high, low = split(kernel_ref[...] * residual_ref[...])
    segment = segment_ref[...]
    spare = jnp.zeros((half - levels - 1, count), F32)
    seg_high = (segment // CLAT * CLAT).astype(F32)
    seg_low = (segment % CLAT).astype(F32)
    data_ref[0:half] = jnp.concatenate(
        [high.astype(F32), seg_high, spare], axis=0).astype(BF16)
    data_ref[half:] = jnp.concatenate(
        [low.astype(F32), seg_low, spare], axis=0).astype(BF16)

    names = lax.broadcasted_iota(jnp.int32, (owners, CHUNK), 0)
    earlier = (lax.broadcasted_iota(jnp.int32, (CHUNK, CHUNK), 0)
               < lax.broadcasted_iota(jnp.int32, (CHUNK, CHUNK), 1)).astype(F32).astype(BF16)
    totals = jnp.zeros((owners, 1), F32)
    for c in range(chunks):
        own = (owner_ref[:, c * CHUNK:(c + 1) * CHUNK] == names).astype(F32)
        totals = totals + jnp.sum(own, axis=1, keepdims=True)
    before = (lax.broadcasted_iota(jnp.int32, (owners, owners), 1)
              < lax.broadcasted_iota(jnp.int32, (owners, owners), 0)).astype(F32)
    carry = jnp.dot(before, jnp.broadcast_to(totals, (owners, CHUNK)),
                    precision=lax.Precision.HIGHEST, preferred_element_type=F32)[:, 0:1]
    for c in range(chunks):
        own = (owner_ref[:, c * CHUNK:(c + 1) * CHUNK] == names).astype(F32)
        inside = jnp.dot(own.astype(BF16), earlier, preferred_element_type=F32)
        place_ref[:, c * CHUNK:(c + 1) * CHUNK] = jnp.sum(
            own * (inside + carry), axis=0, keepdims=True).astype(jnp.int32)
        carry = carry + jnp.sum(own, axis=1, keepdims=True)

    def arrange(block, _):
        base = block * CHUNK
        target = lax.broadcasted_iota(jnp.int32, (CHUNK, count), 0) + base
        chosen = (target == place_ref[...]).astype(F32).astype(BF16)
        got = lax.dot_general(data_ref[...], chosen, NT, preferred_element_type=F32)
        sorted_ref[:, pl.ds(pl.multiple_of(base, CHUNK), CHUNK)] = got[0:ROWS] + got[half:half + ROWS]
        return 0

    lax.fori_loop(0, chunks, arrange, 0)
    sorted_ref[:, count:] = jnp.zeros((ROWS, sorted_ref.shape[1] - count), F32)
    window = capacity + CLAT
    slot = lax.broadcasted_iota(jnp.int32, (ROWS, capacity), 1)
    row = lax.broadcasted_iota(jnp.int32, (ROWS, capacity), 0)

    def hand_out(name, _):
        start = starts_ref[name]
        length = starts_ref[name + 1] - start
        aligned = start // CLAT * CLAT
        run = sorted_ref[:, pl.ds(pl.multiple_of(aligned, CLAT), window)]
        run = pltpu.roll(run, lax.rem(window - (start - aligned), window), 1)[:, 0:capacity]
        out_ref[name] = jnp.where((row == levels) & (slot >= length), -1.0, run)[0:levels + 1]
        return 0

    lax.fori_loop(0, owners, hand_out, 0)


def pack(kernel, residual, owner_block, column, time_step, owners, capacity):
    levels, count = kernel.shape
    owner = owner_block.reshape(1, count)
    segment = (time_step * CELLS + column).reshape(1, count)
    labels = jnp.arange(owners + 1, dtype=jnp.int32)
    starts = jnp.sum((owner < labels[:, None]).astype(jnp.int32), axis=1)
    vmem = pl.BlockSpec(memory_space=pltpu.VMEM)
    return pl.pallas_call(
        functools.partial(pack_kernel, owners, capacity),
        out_shape=jax.ShapeDtypeStruct((owners, levels + 1, capacity), F32),
        in_specs=[pl.BlockSpec(memory_space=pltpu.SMEM)] + [vmem] * 4,
        out_specs=vmem,
        scratch_shapes=[
            pltpu.VMEM((64, count), BF16),
            pltpu.VMEM((1, count), jnp.int32),
            pltpu.VMEM((ROWS, count + capacity + CLAT), F32),
        ],
        compiler_params=pltpu.CompilerParams(vmem_limit_bytes=VMEM_LIMIT),
    )(starts, kernel, residual.reshape(1, count), owner, segment)


def bin_kernel(levels, lons, lats, slots_ref, out_ref, got_ref, total_ref, send_sem, recv_sem):
    owners, _, capacity = slots_ref.shape
    lon, lat = lax.axis_index("lon"), lax.axis_index("lat")
    mesh_id = pl.DeviceIdType.MESH
    half = STEPS * ROWS
    width = min(capacity, 2 * CHUNK)

    def peer(d):
        return lax.rem(lon + d // lats, lons), lax.rem(lat + lax.rem(d, lats), lats)

    def slot_copy(d):
        to_lon, to_lat = peer(d)
        return pltpu.make_async_remote_copy(
            src_ref=slots_ref.at[to_lon * lats + to_lat], dst_ref=got_ref.at[d],
            send_sem=send_sem.at[d], recv_sem=recv_sem.at[d],
            device_id={"lon": to_lon, "lat": to_lat}, device_id_type=mesh_id)

    barrier = pltpu.get_barrier_semaphore()

    def greet(d, _):
        to_lon, to_lat = peer(d)
        pl.semaphore_signal(barrier, inc=1, device_id={"lon": to_lon, "lat": to_lat},
                            device_id_type=mesh_id)
        return 0

    lax.fori_loop(1, owners, greet, 0)
    pl.semaphore_wait(barrier, owners - 1)

    def begin(d, _):
        slot_copy(d).start()
        return 0

    lax.fori_loop(1, owners, begin, 0)
    total_ref[...] = jnp.zeros_like(total_ref)
    got_ref[0] = slots_ref[lon * lats + lat]

    def collect(d, _):
        @pl.when(d > 0)
        def _():
            slot_copy(d).wait_recv()

        for piece in range(capacity // width):
            rows = got_ref[d, :, piece * width:(piece + 1) * width]
            segment = rows[levels:levels + 1].astype(jnp.int32)
            values = jnp.concatenate(
                [rows[0:levels], jnp.zeros((ROWS - levels, width), F32)], axis=0)
            step = jnp.broadcast_to(segment >> 10, (ROWS, width))
            cell = segment & (CELLS - 1)
            place = lax.broadcasted_iota(jnp.int32, (CELLS, width), 0)
            chosen = (place == cell).astype(F32).astype(BF16)
            taken = jnp.concatenate(
                [jnp.where(step == j, values, 0.0) for j in range(STEPS)], axis=0)
            high = taken.astype(BF16)
            low = (taken - high.astype(F32)).astype(BF16)
            total_ref[...] += lax.dot_general(
                jnp.concatenate([high, low], axis=0), chosen, NT, preferred_element_type=F32)
        return 0

    lax.fori_loop(0, owners, collect, 0)
    for i in range(CLON):
        part = (total_ref[0:half, i * CLAT:(i + 1) * CLAT]
                + total_ref[half:, i * CLAT:(i + 1) * CLAT])
        for j in range(STEPS):
            out_ref[j, :, i, :] = part[j * ROWS:j * ROWS + levels]

    def finish(d, _):
        slot_copy(d).wait_send()
        return 0

    lax.fori_loop(1, owners, finish, 0)


def bin_soundings(slots, levels):
    lons, lats = lax.axis_size("lon"), lax.axis_size("lat")
    vmem = pl.BlockSpec(memory_space=pltpu.VMEM)
    return pl.pallas_call(
        functools.partial(bin_kernel, levels, lons, lats),
        out_shape=jax.ShapeDtypeStruct((STEPS, levels, CLON, CLAT), F32),
        in_specs=[vmem],
        out_specs=vmem,
        scratch_shapes=[
            pltpu.VMEM(slots.shape, F32),
            pltpu.VMEM((2 * STEPS * ROWS, CELLS), F32),
            pltpu.SemaphoreType.DMA((lons * lats,)),
            pltpu.SemaphoreType.DMA((lons * lats,)),
        ],
        compiler_params=pltpu.CompilerParams(
            collective_id=1, has_side_effects=True, vmem_limit_bytes=VMEM_LIMIT),
    )(slots)


def steps_kernel(orbits, lons, lats, weights, bins_ref, horizontal_ref, vertical_ref,
                 adjoint_ref, flux_ref, other_ref, forced_ref, mixed_ref, diagonal_ref, weight_ref,
                 edge_ref, lon_out, lon_in, lat_out, lat_in,
                 orbit_send, orbit_recv, edge_send, edge_recv):
    levels = adjoint_ref.shape[0]
    lon, lat, orbit = lax.axis_index("lon"), lax.axis_index("lat"), lax.axis_index("orbit")
    east, west = lax.rem(lon + 1, lons), lax.rem(lon + lons - 1, lons)
    partner = 1 - orbit
    mesh_id = pl.DeviceIdType.MESH
    barrier = pltpu.get_barrier_semaphore()
    pl.semaphore_signal(barrier, inc=1, device_id={"lon": east}, device_id_type=mesh_id)
    pl.semaphore_signal(barrier, inc=1, device_id={"lon": west}, device_id_type=mesh_id)
    pl.semaphore_signal(barrier, inc=1, device_id={"orbit": partner}, device_id_type=mesh_id)

    @pl.when(lat < lats - 1)
    def _():
        pl.semaphore_signal(barrier, inc=1, device_id={"lat": lat + 1}, device_id_type=mesh_id)

    @pl.when(lat > 0)
    def _():
        pl.semaphore_signal(barrier, inc=1, device_id={"lat": lat - 1}, device_id_type=mesh_id)

    peers = 3 + jnp.where(lat > 0, 1, 0) + jnp.where(lat < lats - 1, 1, 0)
    pl.semaphore_wait(barrier, peers)

    def orbit_copy(j):
        return pltpu.make_async_remote_copy(
            src_ref=bins_ref.at[j], dst_ref=other_ref.at[j],
            send_sem=orbit_send.at[j], recv_sem=orbit_recv.at[j],
            device_id={"orbit": partner}, device_id_type=mesh_id)

    def edge_copy(t, side):
        out, into = (lon_out, lon_in) if side < 2 else (lat_out, lat_in)
        device = ({"lon": east}, {"lon": west}, {"lat": lat + 1}, {"lat": lat - 1})[side]
        return pltpu.make_async_remote_copy(
            src_ref=out.at[side % 2, t], dst_ref=into.at[side % 2, t],
            send_sem=edge_send.at[side, t], recv_sem=edge_recv.at[side, t],
            device_id=device, device_id_type=mesh_id)

    def begin(t, _):
        orbit_copy(STEPS - 1 - t).start()
        return 0

    lax.fori_loop(0, STEPS, begin, 0)

    @pl.when(lat == 0)
    def _():
        lat_in[0] = jnp.zeros(lat_in.shape[1:], F32)

    @pl.when(lat == lats - 1)
    def _():
        lat_in[1] = jnp.zeros(lat_in.shape[1:], F32)

    part = (8, CLON, CLAT)
    lane = lax.broadcasted_iota(jnp.int32, part, 2)
    sub = lax.broadcasted_iota(jnp.int32, part, 1)
    level = lax.broadcasted_iota(jnp.int32, part, 0)
    chunks = range(0, levels, 8)
    pairs = CLAT // 2

    def gather_edge(total, values, side, first):
        column = values[:, :, CLAT - 1:CLAT] if side == 0 else values[:, :, 0:1]
        where = (2 * first - side) % CLAT
        place = (where + 2 * level) & (CLAT - 1)
        mine = jnp.sum(jnp.where(lane == place, jnp.broadcast_to(column, part), 0.0), axis=0)
        group = first // pairs
        total[group] = mine if total[group] is None else total[group] + mine

    groups = lat_in.shape[2]
    edge_weight = [[None] * groups, [None] * groups]
    for a in chunks:
        here = slice(a, a + 8)
        h = [horizontal_ref[d, here] for d in range(4)]
        diagonal_ref[here] = 1.0 - h[0] - h[1] - h[2] - h[3]
        weight_ref[0, here] = jnp.where(sub == 0, 0.0, pltpu.roll(h[0], 1, 1))
        weight_ref[1, here] = jnp.where(sub == CLON - 1, 0.0, pltpu.roll(h[1], CLON - 1, 1))
        weight_ref[2, here] = jnp.where(lane == 0, 0.0, pltpu.roll(h[2], 1, 2))
        weight_ref[3, here] = jnp.where(lane == CLAT - 1, 0.0, pltpu.roll(h[3], CLAT - 1, 2))
        gather_edge(edge_weight[0], h[2], 0, a)
        gather_edge(edge_weight[1], h[3], 1, a)
    for side in range(2):
        for g in range(groups):
            edge_ref[side, g] = edge_weight[side][g]

    def force(bins, a):
        forcing = []
        for l in range(a, a + 8):
            parts = [bins[k:k + 1] * float(weights[l, k]) for k in np.nonzero(weights[l])[0]]
            forcing.append(functools.reduce(lambda x, y: x + y, parts))
        return jnp.concatenate(forcing, axis=0)

    orbit_copy(STEPS - 1).wait_recv()
    bins = bins_ref[STEPS - 1] + other_ref[STEPS - 1]
    for a in chunks:
        forced_ref[a:a + 8] = force(bins, a)
    flux_ref[...] = jnp.zeros_like(flux_ref)
    none = jnp.zeros((1, CLON, CLAT), F32)

    def advance(t, _):
        edges = [[None] * groups, [None] * groups]
        for a in chunks:
            low, high = max(a - 1, 0), min(a + 9, levels)
            forced = forced_ref[low:high]
            up = vertical_ref[low:high - 1] * (forced[1:] - forced[:-1])
            if a == 0:
                up = jnp.concatenate([none, up], axis=0)
            if a + 8 == levels:
                up = jnp.concatenate([up, none], axis=0)
            mixed = forced_ref[a:a + 8] + up[1:] - up[:-1]
            mixed_ref[a:a + 8] = mixed
            gather_edge(edges[0], mixed, 0, a)
            gather_edge(edges[1], mixed, 1, a)
        lon_out[0, t] = horizontal_ref[0, :, CLON - 1, :] * mixed_ref[:, CLON - 1, :]
        edge_copy(t, 0).start()
        lon_out[1, t] = horizontal_ref[1, :, 0, :] * mixed_ref[:, 0, :]
        edge_copy(t, 1).start()
        for side in range(2):
            for g in range(groups):
                lat_out[side, t, g] = edge_ref[side, g] * edges[side][g]

        @pl.when(lat < lats - 1)
        def _():
            edge_copy(t, 2).start()

        @pl.when(lat > 0)
        def _():
            edge_copy(t, 3).start()

        for a in chunks:
            here = slice(a, a + 8)
            mixed = mixed_ref[here]
            adjoint_ref[here] = (diagonal_ref[here] * mixed
                                 + weight_ref[0, here] * pltpu.roll(mixed, 1, 1)
                                 + weight_ref[1, here] * pltpu.roll(mixed, CLON - 1, 1)
                                 + weight_ref[2, here] * pltpu.roll(mixed, 1, 2)
                                 + weight_ref[3, here] * pltpu.roll(mixed, CLAT - 1, 2))

        j = jnp.maximum(STEPS - 2 - t, 0)

        @pl.when(t < STEPS - 1)
        def _():
            orbit_copy(j).wait_recv()

        @pl.when(lat > 0)
        def _():
            edge_copy(t, 2).wait_recv()

        @pl.when(lat < lats - 1)
        def _():
            edge_copy(t, 3).wait_recv()

        edge_copy(t, 0).wait_recv()
        edge_copy(t, 1).wait_recv()
        adjoint_ref[:, 0, :] = adjoint_ref[:, 0, :] + lon_in[0, t]
        adjoint_ref[:, CLON - 1, :] = adjoint_ref[:, CLON - 1, :] + lon_in[1, t]
        bins = bins_ref[j] + other_ref[j]
        sides = [lat_in[0, t, g] + lat_in[1, t, g] for g in range(groups)]
        outer = (lane == 0) | (lane == CLAT - 1)
        for a in chunks:
            near = jnp.stack([pltpu.roll(sides[l // pairs], -2 * l % CLAT, 1)
                              for l in range(a, a + 8)])
            result = adjoint_ref[a:a + 8] + jnp.where(outer, near, 0.0)
            adjoint_ref[a:a + 8] = result
            forced_ref[a:a + 8] = result + force(bins, a)
            if a == 0:
                flux_ref[...] += result[0]
        return 0

    lax.fori_loop(0, STEPS, advance, 0)

    def finish(t, _):
        orbit_copy(t).wait_send()
        edge_copy(t, 0).wait_send()
        edge_copy(t, 1).wait_send()

        @pl.when(lat < lats - 1)
        def _():
            edge_copy(t, 2).wait_send()

        @pl.when(lat > 0)
        def _():
            edge_copy(t, 3).wait_send()

        return 0

    lax.fori_loop(0, STEPS, finish, 0)


def transport(bins, horizontal, vertical):
    levels = horizontal.shape[1]
    kernel_levels = bins.shape[1]
    orbits, lons, lats = (lax.axis_size(name) for name in ("orbit", "lon", "lat"))
    vmem = pl.BlockSpec(memory_space=pltpu.VMEM)
    block = (levels, CLON, CLAT)
    groups = -(-2 * levels // CLAT)
    return pl.pallas_call(
        functools.partial(steps_kernel, orbits, lons, lats, level_weights(levels, kernel_levels)),
        out_shape=(jax.ShapeDtypeStruct(block, F32), jax.ShapeDtypeStruct((CLON, CLAT), F32)),
        in_specs=[vmem] * 3,
        out_specs=(vmem, vmem),
        scratch_shapes=[
            pltpu.VMEM(bins.shape, F32),
            pltpu.VMEM(block, F32),
            pltpu.VMEM(block, F32),
            pltpu.VMEM(block, F32),
            pltpu.VMEM((4,) + block, F32),
            pltpu.VMEM((2, groups, CLON, CLAT), F32),
            pltpu.VMEM((2, STEPS, levels, CLAT), F32),
            pltpu.VMEM((2, STEPS, levels, CLAT), F32),
            pltpu.VMEM((2, STEPS, groups, CLON, CLAT), F32),
            pltpu.VMEM((2, STEPS, groups, CLON, CLAT), F32),
            pltpu.SemaphoreType.DMA((STEPS,)),
            pltpu.SemaphoreType.DMA((STEPS,)),
            pltpu.SemaphoreType.DMA((4, STEPS)),
            pltpu.SemaphoreType.DMA((4, STEPS)),
        ],
        compiler_params=pltpu.CompilerParams(
            collective_id=0, has_side_effects=True, vmem_limit_bytes=VMEM_LIMIT),
    )(bins, horizontal, vertical)


def per_device(kernel, residual, owner_block, column, time_step, horizontal, vertical):
    owners = lax.axis_size("lon") * lax.axis_size("lat")
    capacity = 4 * kernel.shape[1] // owners
    slots = pack(kernel, residual, owner_block, column, time_step, owners, capacity)
    return transport(bin_soundings(slots, kernel.shape[0]), horizontal, vertical)


def solution(mesh):
    placed = (
        P(None, ("orbit", "lon", "lat")),
        P(("orbit", "lon", "lat")),
        P(("orbit", "lon", "lat"), None),
        P(("orbit", "lon", "lat")),
        P(("orbit", "lon", "lat")),
        P(None, None, "lon", "lat"),
        P(None, "lon", "lat"),
    )
    return jax.shard_map(
        per_device,
        mesh=mesh,
        in_specs=placed,
        out_specs=(P(None, "lon", "lat"), P("lon", "lat")),
        check_vma=False,
    )
```

```python
import functools

import jax
import jax.numpy as jnp
import numpy as np
from jax import lax
from jax.experimental import pallas as pl
from jax.experimental.pallas import tpu as pltpu
from jax.sharding import PartitionSpec as P

STEPS = 8
CLON = 8
CLAT = 128
CELLS = CLON * CLAT
ROWS = 24
CHUNK = 256
AHEAD = 2
F32 = jnp.float32
BF16 = jnp.bfloat16
VMEM_LIMIT = 48 * 1024 * 1024
NT = (((1,), (1,)), ((), ()))


def level_weights(levels, kernel_levels):
    one = np.float32
    heights = np.arange(levels, dtype=np.float32)
    centre = np.clip((heights + one(0.5)) * one(kernel_levels) / one(levels) - one(0.5),
                     one(0), one(kernel_levels - 1))
    knots = np.arange(kernel_levels, dtype=np.float32)
    return np.maximum(one(0), one(1) - np.abs(centre[:, None] - knots[None, :]))


def split(values):
    high = values.astype(BF16)
    return high, (values - high.astype(F32)).astype(BF16)


def pack_kernel(owners, capacity, starts_ref, kernel_ref, residual_ref, owner_ref, segment_ref,
                out_ref, data_ref, place_ref, sorted_ref):
    levels, count = kernel_ref.shape
    chunks = count // CHUNK
    half = data_ref.shape[0] // 2
    high, low = split(kernel_ref[...] * residual_ref[...])
    segment = segment_ref[...]
    spare = jnp.zeros((half - levels - 1, count), F32)
    seg_high = (segment // CLAT * CLAT).astype(F32)
    seg_low = (segment % CLAT).astype(F32)
    data_ref[0:half] = jnp.concatenate(
        [high.astype(F32), seg_high, spare], axis=0).astype(BF16)
    data_ref[half:] = jnp.concatenate(
        [low.astype(F32), seg_low, spare], axis=0).astype(BF16)

    names = lax.broadcasted_iota(jnp.int32, (owners, CHUNK), 0)
    earlier = (lax.broadcasted_iota(jnp.int32, (CHUNK, CHUNK), 0)
               < lax.broadcasted_iota(jnp.int32, (CHUNK, CHUNK), 1)).astype(F32).astype(BF16)
    totals = jnp.zeros((owners, 1), F32)
    for c in range(chunks):
        own = (owner_ref[:, c * CHUNK:(c + 1) * CHUNK] == names).astype(F32)
        totals = totals + jnp.sum(own, axis=1, keepdims=True)
    before = (lax.broadcasted_iota(jnp.int32, (owners, owners), 1)
              < lax.broadcasted_iota(jnp.int32, (owners, owners), 0)).astype(F32)
    carry = jnp.dot(before, jnp.broadcast_to(totals, (owners, CHUNK)),
                    precision=lax.Precision.HIGHEST, preferred_element_type=F32)[:, 0:1]
    for c in range(chunks):
        own = (owner_ref[:, c * CHUNK:(c + 1) * CHUNK] == names).astype(F32)
        inside = jnp.dot(own.astype(BF16), earlier, preferred_element_type=F32)
        place_ref[:, c * CHUNK:(c + 1) * CHUNK] = jnp.sum(
            own * (inside + carry), axis=0, keepdims=True).astype(jnp.int32)
        carry = carry + jnp.sum(own, axis=1, keepdims=True)

    def arrange(block, _):
        base = block * CHUNK
        target = lax.broadcasted_iota(jnp.int32, (CHUNK, count), 0) + base
        chosen = (target == place_ref[...]).astype(F32).astype(BF16)
        got = lax.dot_general(data_ref[...], chosen, NT, preferred_element_type=F32)
        sorted_ref[:, pl.ds(pl.multiple_of(base, CHUNK), CHUNK)] = got[0:ROWS] + got[half:half + ROWS]
        return 0

    lax.fori_loop(0, chunks, arrange, 0)
    sorted_ref[:, count:] = jnp.zeros((ROWS, sorted_ref.shape[1] - count), F32)
    window = capacity + CLAT
    slot = lax.broadcasted_iota(jnp.int32, (ROWS, capacity), 1)
    row = lax.broadcasted_iota(jnp.int32, (ROWS, capacity), 0)

    def hand_out(name, _):
        start = starts_ref[name]
        length = starts_ref[name + 1] - start
        aligned = start // CLAT * CLAT
        run = sorted_ref[:, pl.ds(pl.multiple_of(aligned, CLAT), window)]
        run = pltpu.roll(run, lax.rem(window - (start - aligned), window), 1)[:, 0:capacity]
        out_ref[name] = jnp.where((row == levels) & (slot >= length), -1.0, run)[0:levels + 1]
        return 0

    lax.fori_loop(0, owners, hand_out, 0)


def pack(kernel, residual, owner_block, column, time_step, owners, capacity):
    levels, count = kernel.shape
    owner = owner_block.reshape(1, count)
    segment = (time_step * CELLS + column).reshape(1, count)
    labels = jnp.arange(owners + 1, dtype=jnp.int32)
    starts = jnp.sum((owner < labels[:, None]).astype(jnp.int32), axis=1)
    vmem = pl.BlockSpec(memory_space=pltpu.VMEM)
    return pl.pallas_call(
        functools.partial(pack_kernel, owners, capacity),
        out_shape=jax.ShapeDtypeStruct((owners, levels + 1, capacity), F32),
        in_specs=[pl.BlockSpec(memory_space=pltpu.SMEM)] + [vmem] * 4,
        out_specs=vmem,
        scratch_shapes=[
            pltpu.VMEM((64, count), BF16),
            pltpu.VMEM((1, count), jnp.int32),
            pltpu.VMEM((ROWS, count + capacity + CLAT), F32),
        ],
        compiler_params=pltpu.CompilerParams(vmem_limit_bytes=VMEM_LIMIT),
    )(starts, kernel, residual.reshape(1, count), owner, segment)


def bin_kernel(levels, lons, lats, slots_ref, out_ref, got_ref, total_ref, send_sem, recv_sem):
    owners, _, capacity = slots_ref.shape
    lon, lat = lax.axis_index("lon"), lax.axis_index("lat")
    mesh_id = pl.DeviceIdType.MESH
    half = STEPS * ROWS
    width = min(capacity, 2 * CHUNK)

    def peer(d):
        return lax.rem(lon + d // lats, lons), lax.rem(lat + lax.rem(d, lats), lats)

    def slot_copy(d):
        to_lon, to_lat = peer(d)
        return pltpu.make_async_remote_copy(
            src_ref=slots_ref.at[to_lon * lats + to_lat], dst_ref=got_ref.at[d],
            send_sem=send_sem.at[d], recv_sem=recv_sem.at[d],
            device_id={"lon": to_lon, "lat": to_lat}, device_id_type=mesh_id)

    barrier = pltpu.get_barrier_semaphore()

    def greet(d, _):
        to_lon, to_lat = peer(d)
        pl.semaphore_signal(barrier, inc=1, device_id={"lon": to_lon, "lat": to_lat},
                            device_id_type=mesh_id)
        return 0

    lax.fori_loop(1, owners, greet, 0)
    pl.semaphore_wait(barrier, owners - 1)

    def begin(d, _):
        slot_copy(d).start()
        return 0

    lax.fori_loop(1, owners, begin, 0)
    total_ref[...] = jnp.zeros_like(total_ref)
    got_ref[0] = slots_ref[lon * lats + lat]

    def collect(d, _):
        @pl.when(d > 0)
        def _():
            slot_copy(d).wait_recv()

        for piece in range(capacity // width):
            rows = got_ref[d, :, piece * width:(piece + 1) * width]
            segment = rows[levels:levels + 1].astype(jnp.int32)
            values = jnp.concatenate(
                [rows[0:levels], jnp.zeros((ROWS - levels, width), F32)], axis=0)
            step = jnp.broadcast_to(segment >> 10, (ROWS, width))
            cell = segment & (CELLS - 1)
            place = lax.broadcasted_iota(jnp.int32, (CELLS, width), 0)
            chosen = (place == cell).astype(F32).astype(BF16)
            taken = jnp.concatenate(
                [jnp.where(step == j, values, 0.0) for j in range(STEPS)], axis=0)
            high = taken.astype(BF16)
            low = (taken - high.astype(F32)).astype(BF16)
            total_ref[...] += lax.dot_general(
                jnp.concatenate([high, low], axis=0), chosen, NT, preferred_element_type=F32)
        return 0

    lax.fori_loop(0, owners, collect, 0)
    for i in range(CLON):
        part = (total_ref[0:half, i * CLAT:(i + 1) * CLAT]
                + total_ref[half:, i * CLAT:(i + 1) * CLAT])
        for j in range(STEPS):
            out_ref[j, :, i, :] = part[j * ROWS:j * ROWS + levels]

    def finish(d, _):
        slot_copy(d).wait_send()
        return 0

    lax.fori_loop(1, owners, finish, 0)


def bin_soundings(slots, levels):
    lons, lats = lax.axis_size("lon"), lax.axis_size("lat")
    vmem = pl.BlockSpec(memory_space=pltpu.VMEM)
    return pl.pallas_call(
        functools.partial(bin_kernel, levels, lons, lats),
        out_shape=jax.ShapeDtypeStruct((STEPS, levels, CLON, CLAT), F32),
        in_specs=[vmem],
        out_specs=vmem,
        scratch_shapes=[
            pltpu.VMEM(slots.shape, F32),
            pltpu.VMEM((2 * STEPS * ROWS, CELLS), F32),
            pltpu.SemaphoreType.DMA((lons * lats,)),
            pltpu.SemaphoreType.DMA((lons * lats,)),
        ],
        compiler_params=pltpu.CompilerParams(
            collective_id=1, has_side_effects=True, vmem_limit_bytes=VMEM_LIMIT),
    )(slots)


def steps_kernel(orbits, lons, lats, weights, bins_ref, horizontal_ref, vertical_ref,
                 adjoint_ref, flux_ref, other_ref, forced_ref, mixed_ref, diagonal_ref, weight_ref,
                 edge_ref, lon_out, lon_in, lat_out, lat_in,
                 orbit_send, orbit_recv, edge_send, edge_recv):
    levels = adjoint_ref.shape[0]
    lon, lat, orbit = lax.axis_index("lon"), lax.axis_index("lat"), lax.axis_index("orbit")
    east, west = lax.rem(lon + 1, lons), lax.rem(lon + lons - 1, lons)
    partner = 1 - orbit
    mesh_id = pl.DeviceIdType.MESH
    barrier = pltpu.get_barrier_semaphore()
    pl.semaphore_signal(barrier, inc=1, device_id={"lon": east}, device_id_type=mesh_id)
    pl.semaphore_signal(barrier, inc=1, device_id={"lon": west}, device_id_type=mesh_id)
    pl.semaphore_signal(barrier, inc=1, device_id={"orbit": partner}, device_id_type=mesh_id)

    @pl.when(lat < lats - 1)
    def _():
        pl.semaphore_signal(barrier, inc=1, device_id={"lat": lat + 1}, device_id_type=mesh_id)

    @pl.when(lat > 0)
    def _():
        pl.semaphore_signal(barrier, inc=1, device_id={"lat": lat - 1}, device_id_type=mesh_id)

    peers = 3 + jnp.where(lat > 0, 1, 0) + jnp.where(lat < lats - 1, 1, 0)
    pl.semaphore_wait(barrier, peers)

    def orbit_copy(j):
        return pltpu.make_async_remote_copy(
            src_ref=bins_ref.at[j], dst_ref=other_ref.at[j],
            send_sem=orbit_send.at[j], recv_sem=orbit_recv.at[j],
            device_id={"orbit": partner}, device_id_type=mesh_id)

    def edge_copy(t, side):
        out, into = (lon_out, lon_in) if side < 2 else (lat_out, lat_in)
        device = ({"lon": east}, {"lon": west}, {"lat": lat + 1}, {"lat": lat - 1})[side]
        return pltpu.make_async_remote_copy(
            src_ref=out.at[side % 2, t], dst_ref=into.at[side % 2, t],
            send_sem=edge_send.at[side, t], recv_sem=edge_recv.at[side, t],
            device_id=device, device_id_type=mesh_id)

    def begin(t, _):
        orbit_copy(STEPS - 1 - t).start()
        return 0

    lax.fori_loop(0, AHEAD, begin, 0)

    @pl.when(lat == 0)
    def _():
        lat_in[0] = jnp.zeros(lat_in.shape[1:], F32)

    @pl.when(lat == lats - 1)
    def _():
        lat_in[1] = jnp.zeros(lat_in.shape[1:], F32)

    part = (8, CLON, CLAT)
    lane = lax.broadcasted_iota(jnp.int32, part, 2)
    sub = lax.broadcasted_iota(jnp.int32, part, 1)
    level = lax.broadcasted_iota(jnp.int32, part, 0)
    chunks = range(0, levels, 8)
    pairs = CLAT // 2

    def gather_edge(total, values, side, first):
        column = values[:, :, CLAT - 1:CLAT] if side == 0 else values[:, :, 0:1]
        where = (2 * first - side) % CLAT
        place = (where + 2 * level) & (CLAT - 1)
        mine = jnp.sum(jnp.where(lane == place, jnp.broadcast_to(column, part), 0.0), axis=0)
        group = first // pairs
        total[group] = mine if total[group] is None else total[group] + mine

    groups = lat_in.shape[2]
    edge_weight = [[None] * groups, [None] * groups]
    for a in chunks:
        here = slice(a, a + 8)
        h = [horizontal_ref[d, here] for d in range(4)]
        diagonal_ref[here] = 1.0 - h[0] - h[1] - h[2] - h[3]
        weight_ref[0, here] = jnp.where(sub == 0, 0.0, pltpu.roll(h[0], 1, 1))
        weight_ref[1, here] = jnp.where(sub == CLON - 1, 0.0, pltpu.roll(h[1], CLON - 1, 1))
        weight_ref[2, here] = jnp.where(lane == 0, 0.0, pltpu.roll(h[2], 1, 2))
        weight_ref[3, here] = jnp.where(lane == CLAT - 1, 0.0, pltpu.roll(h[3], CLAT - 1, 2))
        gather_edge(edge_weight[0], h[2], 0, a)
        gather_edge(edge_weight[1], h[3], 1, a)
    for side in range(2):
        for g in range(groups):
            edge_ref[side, g] = edge_weight[side][g]

    def force(bins, a):
        forcing = []
        for l in range(a, a + 8):
            parts = [bins[k:k + 1] * float(weights[l, k]) for k in np.nonzero(weights[l])[0]]
            forcing.append(functools.reduce(lambda x, y: x + y, parts))
        return jnp.concatenate(forcing, axis=0)

    orbit_copy(STEPS - 1).wait_recv()
    bins = bins_ref[STEPS - 1] + other_ref[STEPS - 1]
    for a in chunks:
        forced_ref[a:a + 8] = force(bins, a)
    flux_ref[...] = jnp.zeros_like(flux_ref)
    none = jnp.zeros((1, CLON, CLAT), F32)

    def advance(t, _):
        edges = [[None] * groups, [None] * groups]
        for a in chunks:
            low, high = max(a - 1, 0), min(a + 9, levels)
            forced = forced_ref[low:high]
            up = vertical_ref[low:high - 1] * (forced[1:] - forced[:-1])
            if a == 0:
                up = jnp.concatenate([none, up], axis=0)
            if a + 8 == levels:
                up = jnp.concatenate([up, none], axis=0)
            mixed = forced_ref[a:a + 8] + up[1:] - up[:-1]
            mixed_ref[a:a + 8] = mixed
            gather_edge(edges[0], mixed, 0, a)
            gather_edge(edges[1], mixed, 1, a)
        lon_out[0, t] = horizontal_ref[0, :, CLON - 1, :] * mixed_ref[:, CLON - 1, :]
        edge_copy(t, 0).start()
        lon_out[1, t] = horizontal_ref[1, :, 0, :] * mixed_ref[:, 0, :]
        edge_copy(t, 1).start()
        for side in range(2):
            for g in range(groups):
                lat_out[side, t, g] = edge_ref[side, g] * edges[side][g]

        @pl.when(lat < lats - 1)
        def _():
            edge_copy(t, 2).start()

        @pl.when(lat > 0)
        def _():
            edge_copy(t, 3).start()

        @pl.when(t < STEPS - AHEAD)
        def _():
            orbit_copy(jnp.maximum(STEPS - 1 - AHEAD - t, 0)).start()

        for a in chunks:
            here = slice(a, a + 8)
            mixed = mixed_ref[here]
            adjoint_ref[here] = (diagonal_ref[here] * mixed
                                 + weight_ref[0, here] * pltpu.roll(mixed, 1, 1)
                                 + weight_ref[1, here] * pltpu.roll(mixed, CLON - 1, 1)
                                 + weight_ref[2, here] * pltpu.roll(mixed, 1, 2)
                                 + weight_ref[3, here] * pltpu.roll(mixed, CLAT - 1, 2))

        j = jnp.maximum(STEPS - 2 - t, 0)

        @pl.when(t < STEPS - 1)
        def _():
            orbit_copy(j).wait_recv()

        @pl.when(lat > 0)
        def _():
            edge_copy(t, 2).wait_recv()

        @pl.when(lat < lats - 1)
        def _():
            edge_copy(t, 3).wait_recv()

        edge_copy(t, 0).wait_recv()
        edge_copy(t, 1).wait_recv()
        adjoint_ref[:, 0, :] = adjoint_ref[:, 0, :] + lon_in[0, t]
        adjoint_ref[:, CLON - 1, :] = adjoint_ref[:, CLON - 1, :] + lon_in[1, t]
        bins = bins_ref[j] + other_ref[j]
        sides = [lat_in[0, t, g] + lat_in[1, t, g] for g in range(groups)]
        outer = (lane == 0) | (lane == CLAT - 1)
        for a in chunks:
            near = jnp.stack([pltpu.roll(sides[l // pairs], -2 * l % CLAT, 1)
                              for l in range(a, a + 8)])
            result = adjoint_ref[a:a + 8] + jnp.where(outer, near, 0.0)
            adjoint_ref[a:a + 8] = result
            forced_ref[a:a + 8] = result + force(bins, a)
            if a == 0:
                flux_ref[...] += result[0]
        return 0

    lax.fori_loop(0, STEPS, advance, 0)

    def finish(t, _):
        orbit_copy(t).wait_send()
        edge_copy(t, 0).wait_send()
        edge_copy(t, 1).wait_send()

        @pl.when(lat < lats - 1)
        def _():
            edge_copy(t, 2).wait_send()

        @pl.when(lat > 0)
        def _():
            edge_copy(t, 3).wait_send()

        return 0

    lax.fori_loop(0, STEPS, finish, 0)


def transport(bins, horizontal, vertical):
    levels = horizontal.shape[1]
    kernel_levels = bins.shape[1]
    orbits, lons, lats = (lax.axis_size(name) for name in ("orbit", "lon", "lat"))
    vmem = pl.BlockSpec(memory_space=pltpu.VMEM)
    block = (levels, CLON, CLAT)
    groups = -(-2 * levels // CLAT)
    return pl.pallas_call(
        functools.partial(steps_kernel, orbits, lons, lats, level_weights(levels, kernel_levels)),
        out_shape=(jax.ShapeDtypeStruct(block, F32), jax.ShapeDtypeStruct((CLON, CLAT), F32)),
        in_specs=[vmem] * 3,
        out_specs=(vmem, vmem),
        scratch_shapes=[
            pltpu.VMEM(bins.shape, F32),
            pltpu.VMEM(block, F32),
            pltpu.VMEM(block, F32),
            pltpu.VMEM(block, F32),
            pltpu.VMEM((4,) + block, F32),
            pltpu.VMEM((2, groups, CLON, CLAT), F32),
            pltpu.VMEM((2, STEPS, levels, CLAT), F32),
            pltpu.VMEM((2, STEPS, levels, CLAT), F32),
            pltpu.VMEM((2, STEPS, groups, CLON, CLAT), F32),
            pltpu.VMEM((2, STEPS, groups, CLON, CLAT), F32),
            pltpu.SemaphoreType.DMA((STEPS,)),
            pltpu.SemaphoreType.DMA((STEPS,)),
            pltpu.SemaphoreType.DMA((4, STEPS)),
            pltpu.SemaphoreType.DMA((4, STEPS)),
        ],
        compiler_params=pltpu.CompilerParams(
            collective_id=0, has_side_effects=True, vmem_limit_bytes=VMEM_LIMIT),
    )(bins, horizontal, vertical)


def per_device(kernel, residual, owner_block, column, time_step, horizontal, vertical):
    owners = lax.axis_size("lon") * lax.axis_size("lat")
    capacity = 4 * kernel.shape[1] // owners
    slots = pack(kernel, residual, owner_block, column, time_step, owners, capacity)
    return transport(bin_soundings(slots, kernel.shape[0]), horizontal, vertical)


def solution(mesh):
    placed = (
        P(None, ("orbit", "lon", "lat")),
        P(("orbit", "lon", "lat")),
        P(("orbit", "lon", "lat"), None),
        P(("orbit", "lon", "lat")),
        P(("orbit", "lon", "lat")),
        P(None, None, "lon", "lat"),
        P(None, "lon", "lat"),
    )
    return jax.shard_map(
        per_device,
        mesh=mesh,
        in_specs=placed,
        out_specs=(P(None, "lon", "lat"), P("lon", "lat")),
        check_vma=False,
    )
```

```python
import functools

import jax
import jax.numpy as jnp
import numpy as np
from jax import lax
from jax.experimental import pallas as pl
from jax.experimental.pallas import tpu as pltpu
from jax.sharding import PartitionSpec as P

STEPS = 8
CLON = 8
CLAT = 128
CELLS = CLON * CLAT
ROWS = 24
CHUNK = 256
F32 = jnp.float32
BF16 = jnp.bfloat16
VMEM_LIMIT = 48 * 1024 * 1024
NT = (((1,), (1,)), ((), ()))


def level_weights(levels, kernel_levels):
    one = np.float32
    heights = np.arange(levels, dtype=np.float32)
    centre = np.clip((heights + one(0.5)) * one(kernel_levels) / one(levels) - one(0.5),
                     one(0), one(kernel_levels - 1))
    knots = np.arange(kernel_levels, dtype=np.float32)
    return np.maximum(one(0), one(1) - np.abs(centre[:, None] - knots[None, :]))


def split(values):
    high = values.astype(BF16)
    return high, (values - high.astype(F32)).astype(BF16)


def pack_kernel(owners, capacity, starts_ref, kernel_ref, residual_ref, owner_ref, segment_ref,
                out_ref, data_ref, place_ref, sorted_ref):
    levels, count = kernel_ref.shape
    chunks = count // CHUNK
    half = data_ref.shape[0] // 2
    high, low = split(kernel_ref[...] * residual_ref[...])
    segment = segment_ref[...]
    spare = jnp.zeros((half - levels - 1, count), F32)
    seg_high = (segment // CLAT * CLAT).astype(F32)
    seg_low = (segment % CLAT).astype(F32)
    data_ref[0:half] = jnp.concatenate(
        [high.astype(F32), seg_high, spare], axis=0).astype(BF16)
    data_ref[half:] = jnp.concatenate(
        [low.astype(F32), seg_low, spare], axis=0).astype(BF16)

    names = lax.broadcasted_iota(jnp.int32, (owners, CHUNK), 0)
    earlier = (lax.broadcasted_iota(jnp.int32, (CHUNK, CHUNK), 0)
               < lax.broadcasted_iota(jnp.int32, (CHUNK, CHUNK), 1)).astype(F32).astype(BF16)
    totals = jnp.zeros((owners, 1), F32)
    for c in range(chunks):
        own = (owner_ref[:, c * CHUNK:(c + 1) * CHUNK] == names).astype(F32)
        totals = totals + jnp.sum(own, axis=1, keepdims=True)
    before = (lax.broadcasted_iota(jnp.int32, (owners, owners), 1)
              < lax.broadcasted_iota(jnp.int32, (owners, owners), 0)).astype(F32)
    carry = jnp.dot(before, jnp.broadcast_to(totals, (owners, CHUNK)),
                    precision=lax.Precision.HIGHEST, preferred_element_type=F32)[:, 0:1]
    for c in range(chunks):
        own = (owner_ref[:, c * CHUNK:(c + 1) * CHUNK] == names).astype(F32)
        inside = jnp.dot(own.astype(BF16), earlier, preferred_element_type=F32)
        place_ref[:, c * CHUNK:(c + 1) * CHUNK] = jnp.sum(
            own * (inside + carry), axis=0, keepdims=True).astype(jnp.int32)
        carry = carry + jnp.sum(own, axis=1, keepdims=True)

    def arrange(block, _):
        base = block * CHUNK
        target = lax.broadcasted_iota(jnp.int32, (CHUNK, count), 0) + base
        chosen = (target == place_ref[...]).astype(F32).astype(BF16)
        got = lax.dot_general(data_ref[...], chosen, NT, preferred_element_type=F32)
        sorted_ref[:, pl.ds(pl.multiple_of(base, CHUNK), CHUNK)] = got[0:ROWS] + got[half:half + ROWS]
        return 0

    lax.fori_loop(0, chunks, arrange, 0)
    sorted_ref[:, count:] = jnp.zeros((ROWS, sorted_ref.shape[1] - count), F32)
    window = capacity + CLAT
    slot = lax.broadcasted_iota(jnp.int32, (ROWS, capacity), 1)
    row = lax.broadcasted_iota(jnp.int32, (ROWS, capacity), 0)

    def hand_out(name, _):
        start = starts_ref[name]
        length = starts_ref[name + 1] - start
        aligned = start // CLAT * CLAT
        run = sorted_ref[:, pl.ds(pl.multiple_of(aligned, CLAT), window)]
        run = pltpu.roll(run, lax.rem(window - (start - aligned), window), 1)[:, 0:capacity]
        out_ref[name] = jnp.where((row == levels) & (slot >= length), -1.0, run)[0:levels + 1]
        return 0

    lax.fori_loop(0, owners, hand_out, 0)


def pack(kernel, residual, owner_block, column, time_step, owners, capacity):
    levels, count = kernel.shape
    owner = owner_block.reshape(1, count)
    segment = (time_step * CELLS + column).reshape(1, count)
    labels = jnp.arange(owners + 1, dtype=jnp.int32)
    starts = jnp.sum((owner < labels[:, None]).astype(jnp.int32), axis=1)
    vmem = pl.BlockSpec(memory_space=pltpu.VMEM)
    return pl.pallas_call(
        functools.partial(pack_kernel, owners, capacity),
        out_shape=jax.ShapeDtypeStruct((owners, levels + 1, capacity), F32),
        in_specs=[pl.BlockSpec(memory_space=pltpu.SMEM)] + [vmem] * 4,
        out_specs=vmem,
        scratch_shapes=[
            pltpu.VMEM((64, count), BF16),
            pltpu.VMEM((1, count), jnp.int32),
            pltpu.VMEM((ROWS, count + capacity + CLAT), F32),
        ],
        compiler_params=pltpu.CompilerParams(vmem_limit_bytes=VMEM_LIMIT),
    )(starts, kernel, residual.reshape(1, count), owner, segment)


def bin_kernel(levels, lons, lats, slots_ref, out_ref, got_ref, total_ref, send_sem, recv_sem):
    owners, _, capacity = slots_ref.shape
    lon, lat = lax.axis_index("lon"), lax.axis_index("lat")
    mesh_id = pl.DeviceIdType.MESH
    half = STEPS * ROWS
    width = min(capacity, 2 * CHUNK)

    def peer(d):
        return lax.rem(lon + d // lats, lons), lax.rem(lat + lax.rem(d, lats), lats)

    def slot_copy(d):
        to_lon, to_lat = peer(d)
        return pltpu.make_async_remote_copy(
            src_ref=slots_ref.at[to_lon * lats + to_lat], dst_ref=got_ref.at[d],
            send_sem=send_sem.at[d], recv_sem=recv_sem.at[d],
            device_id={"lon": to_lon, "lat": to_lat}, device_id_type=mesh_id)

    barrier = pltpu.get_barrier_semaphore()

    def greet(d, _):
        to_lon, to_lat = peer(d)
        pl.semaphore_signal(barrier, inc=1, device_id={"lon": to_lon, "lat": to_lat},
                            device_id_type=mesh_id)
        return 0

    lax.fori_loop(1, owners, greet, 0)
    pl.semaphore_wait(barrier, owners - 1)

    def turn(i):
        return jnp.where(lax.rem(i, 2) == 1, (i + 1) // 2, lax.rem(owners - i // 2, owners))

    def begin(i, _):
        slot_copy(turn(i)).start()
        return 0

    lax.fori_loop(1, owners, begin, 0)
    total_ref[...] = jnp.zeros_like(total_ref)
    got_ref[0] = slots_ref[lon * lats + lat]

    def collect(i, _):
        d = turn(i)

        @pl.when(i > 0)
        def _():
            slot_copy(d).wait_recv()

        for piece in range(capacity // width):
            rows = got_ref[d, :, piece * width:(piece + 1) * width]
            segment = rows[levels:levels + 1].astype(jnp.int32)
            values = jnp.concatenate(
                [rows[0:levels], jnp.zeros((ROWS - levels, width), F32)], axis=0)
            step = jnp.broadcast_to(segment >> 10, (ROWS, width))
            cell = segment & (CELLS - 1)
            place = lax.broadcasted_iota(jnp.int32, (CELLS, width), 0)
            chosen = (place == cell).astype(F32).astype(BF16)
            taken = jnp.concatenate(
                [jnp.where(step == j, values, 0.0) for j in range(STEPS)], axis=0)
            high = taken.astype(BF16)
            low = (taken - high.astype(F32)).astype(BF16)
            total_ref[...] += lax.dot_general(
                jnp.concatenate([high, low], axis=0), chosen, NT, preferred_element_type=F32)
        return 0

    lax.fori_loop(0, owners, collect, 0)
    for i in range(CLON):
        part = (total_ref[0:half, i * CLAT:(i + 1) * CLAT]
                + total_ref[half:, i * CLAT:(i + 1) * CLAT])
        for j in range(STEPS):
            out_ref[j, :, i, :] = part[j * ROWS:j * ROWS + levels]

    def finish(d, _):
        slot_copy(d).wait_send()
        return 0

    lax.fori_loop(1, owners, finish, 0)


def bin_soundings(slots, levels):
    lons, lats = lax.axis_size("lon"), lax.axis_size("lat")
    vmem = pl.BlockSpec(memory_space=pltpu.VMEM)
    return pl.pallas_call(
        functools.partial(bin_kernel, levels, lons, lats),
        out_shape=jax.ShapeDtypeStruct((STEPS, levels, CLON, CLAT), F32),
        in_specs=[vmem],
        out_specs=vmem,
        scratch_shapes=[
            pltpu.VMEM(slots.shape, F32),
            pltpu.VMEM((2 * STEPS * ROWS, CELLS), F32),
            pltpu.SemaphoreType.DMA((lons * lats,)),
            pltpu.SemaphoreType.DMA((lons * lats,)),
        ],
        compiler_params=pltpu.CompilerParams(
            collective_id=1, has_side_effects=True, vmem_limit_bytes=VMEM_LIMIT),
    )(slots)


def steps_kernel(orbits, lons, lats, weights, bins_ref, horizontal_ref, vertical_ref,
                 adjoint_ref, flux_ref, other_ref, forced_ref, mixed_ref, diagonal_ref, weight_ref,
                 edge_ref, lon_out, lon_in, lat_out, lat_in,
                 orbit_send, orbit_recv, edge_send, edge_recv):
    levels = adjoint_ref.shape[0]
    lon, lat, orbit = lax.axis_index("lon"), lax.axis_index("lat"), lax.axis_index("orbit")
    east, west = lax.rem(lon + 1, lons), lax.rem(lon + lons - 1, lons)
    partner = 1 - orbit
    mesh_id = pl.DeviceIdType.MESH
    barrier = pltpu.get_barrier_semaphore()
    pl.semaphore_signal(barrier, inc=1, device_id={"lon": east}, device_id_type=mesh_id)
    pl.semaphore_signal(barrier, inc=1, device_id={"lon": west}, device_id_type=mesh_id)
    pl.semaphore_signal(barrier, inc=1, device_id={"orbit": partner}, device_id_type=mesh_id)

    @pl.when(lat < lats - 1)
    def _():
        pl.semaphore_signal(barrier, inc=1, device_id={"lat": lat + 1}, device_id_type=mesh_id)

    @pl.when(lat > 0)
    def _():
        pl.semaphore_signal(barrier, inc=1, device_id={"lat": lat - 1}, device_id_type=mesh_id)

    peers = 3 + jnp.where(lat > 0, 1, 0) + jnp.where(lat < lats - 1, 1, 0)
    pl.semaphore_wait(barrier, peers)

    def orbit_copy(j):
        return pltpu.make_async_remote_copy(
            src_ref=bins_ref.at[j], dst_ref=other_ref.at[j],
            send_sem=orbit_send.at[j], recv_sem=orbit_recv.at[j],
            device_id={"orbit": partner}, device_id_type=mesh_id)

    def edge_copy(t, side):
        out, into = (lon_out, lon_in) if side < 2 else (lat_out, lat_in)
        device = ({"lon": east}, {"lon": west}, {"lat": lat + 1}, {"lat": lat - 1})[side]
        return pltpu.make_async_remote_copy(
            src_ref=out.at[side % 2, t], dst_ref=into.at[side % 2, t],
            send_sem=edge_send.at[side, t], recv_sem=edge_recv.at[side, t],
            device_id=device, device_id_type=mesh_id)

    def begin(t, _):
        orbit_copy(STEPS - 1 - t).start()
        return 0

    lax.fori_loop(0, STEPS, begin, 0)

    @pl.when(lat == 0)
    def _():
        lat_in[0] = jnp.zeros(lat_in.shape[1:], F32)

    @pl.when(lat == lats - 1)
    def _():
        lat_in[1] = jnp.zeros(lat_in.shape[1:], F32)

    part = (8, CLON, CLAT)
    lane = lax.broadcasted_iota(jnp.int32, part, 2)
    sub = lax.broadcasted_iota(jnp.int32, part, 1)
    level = lax.broadcasted_iota(jnp.int32, part, 0)
    chunks = range(0, levels, 8)
    pairs = CLAT // 2

    def gather_edge(total, values, side, first):
        column = values[:, :, CLAT - 1:CLAT] if side == 0 else values[:, :, 0:1]
        where = (2 * first - side) % CLAT
        place = (where + 2 * level) & (CLAT - 1)
        mine = jnp.sum(jnp.where(lane == place, jnp.broadcast_to(column, part), 0.0), axis=0)
        group = first // pairs
        total[group] = mine if total[group] is None else total[group] + mine

    groups = lat_in.shape[2]
    edge_weight = [[None] * groups, [None] * groups]
    for a in chunks:
        here = slice(a, a + 8)
        h = [horizontal_ref[d, here] for d in range(4)]
        diagonal_ref[here] = 1.0 - h[0] - h[1] - h[2] - h[3]
        weight_ref[0, here] = jnp.where(sub == 0, 0.0, pltpu.roll(h[0], 1, 1))
        weight_ref[1, here] = jnp.where(sub == CLON - 1, 0.0, pltpu.roll(h[1], CLON - 1, 1))
        weight_ref[2, here] = jnp.where(lane == 0, 0.0, pltpu.roll(h[2], 1, 2))
        weight_ref[3, here] = jnp.where(lane == CLAT - 1, 0.0, pltpu.roll(h[3], CLAT - 1, 2))
        gather_edge(edge_weight[0], h[2], 0, a)
        gather_edge(edge_weight[1], h[3], 1, a)
    for side in range(2):
        for g in range(groups):
            edge_ref[side, g] = edge_weight[side][g]

    def force(bins, a):
        forcing = []
        for l in range(a, a + 8):
            parts = [bins[k:k + 1] * float(weights[l, k]) for k in np.nonzero(weights[l])[0]]
            forcing.append(functools.reduce(lambda x, y: x + y, parts))
        return jnp.concatenate(forcing, axis=0)

    orbit_copy(STEPS - 1).wait_recv()
    bins = bins_ref[STEPS - 1] + other_ref[STEPS - 1]
    for a in chunks:
        forced_ref[a:a + 8] = force(bins, a)
    flux_ref[...] = jnp.zeros_like(flux_ref)
    none = jnp.zeros((1, CLON, CLAT), F32)

    def advance(t, _):
        edges = [[None] * groups, [None] * groups]
        for a in chunks:
            low, high = max(a - 1, 0), min(a + 9, levels)
            forced = forced_ref[low:high]
            up = vertical_ref[low:high - 1] * (forced[1:] - forced[:-1])
            if a == 0:
                up = jnp.concatenate([none, up], axis=0)
            if a + 8 == levels:
                up = jnp.concatenate([up, none], axis=0)
            mixed = forced_ref[a:a + 8] + up[1:] - up[:-1]
            mixed_ref[a:a + 8] = mixed
            gather_edge(edges[0], mixed, 0, a)
            gather_edge(edges[1], mixed, 1, a)
        lon_out[0, t] = horizontal_ref[0, :, CLON - 1, :] * mixed_ref[:, CLON - 1, :]
        edge_copy(t, 0).start()
        lon_out[1, t] = horizontal_ref[1, :, 0, :] * mixed_ref[:, 0, :]
        edge_copy(t, 1).start()
        for side in range(2):
            for g in range(groups):
                lat_out[side, t, g] = edge_ref[side, g] * edges[side][g]

        @pl.when(lat < lats - 1)
        def _():
            edge_copy(t, 2).start()

        @pl.when(lat > 0)
        def _():
            edge_copy(t, 3).start()

        for a in chunks:
            here = slice(a, a + 8)
            mixed = mixed_ref[here]
            adjoint_ref[here] = (diagonal_ref[here] * mixed
                                 + weight_ref[0, here] * pltpu.roll(mixed, 1, 1)
                                 + weight_ref[1, here] * pltpu.roll(mixed, CLON - 1, 1)
                                 + weight_ref[2, here] * pltpu.roll(mixed, 1, 2)
                                 + weight_ref[3, here] * pltpu.roll(mixed, CLAT - 1, 2))

        j = jnp.maximum(STEPS - 2 - t, 0)

        @pl.when(t < STEPS - 1)
        def _():
            orbit_copy(j).wait_recv()

        @pl.when(lat > 0)
        def _():
            edge_copy(t, 2).wait_recv()

        @pl.when(lat < lats - 1)
        def _():
            edge_copy(t, 3).wait_recv()

        edge_copy(t, 0).wait_recv()
        edge_copy(t, 1).wait_recv()
        adjoint_ref[:, 0, :] = adjoint_ref[:, 0, :] + lon_in[0, t]
        adjoint_ref[:, CLON - 1, :] = adjoint_ref[:, CLON - 1, :] + lon_in[1, t]
        bins = bins_ref[j] + other_ref[j]
        sides = [lat_in[0, t, g] + lat_in[1, t, g] for g in range(groups)]
        outer = (lane == 0) | (lane == CLAT - 1)
        for a in chunks:
            near = jnp.stack([pltpu.roll(sides[l // pairs], -2 * l % CLAT, 1)
                              for l in range(a, a + 8)])
            result = adjoint_ref[a:a + 8] + jnp.where(outer, near, 0.0)
            adjoint_ref[a:a + 8] = result
            forced_ref[a:a + 8] = result + force(bins, a)
            if a == 0:
                flux_ref[...] += result[0]
        return 0

    lax.fori_loop(0, STEPS, advance, 0)

    def finish(t, _):
        orbit_copy(t).wait_send()
        edge_copy(t, 0).wait_send()
        edge_copy(t, 1).wait_send()

        @pl.when(lat < lats - 1)
        def _():
            edge_copy(t, 2).wait_send()

        @pl.when(lat > 0)
        def _():
            edge_copy(t, 3).wait_send()

        return 0

    lax.fori_loop(0, STEPS, finish, 0)


def transport(bins, horizontal, vertical):
    levels = horizontal.shape[1]
    kernel_levels = bins.shape[1]
    orbits, lons, lats = (lax.axis_size(name) for name in ("orbit", "lon", "lat"))
    vmem = pl.BlockSpec(memory_space=pltpu.VMEM)
    block = (levels, CLON, CLAT)
    groups = -(-2 * levels // CLAT)
    return pl.pallas_call(
        functools.partial(steps_kernel, orbits, lons, lats, level_weights(levels, kernel_levels)),
        out_shape=(jax.ShapeDtypeStruct(block, F32), jax.ShapeDtypeStruct((CLON, CLAT), F32)),
        in_specs=[vmem] * 3,
        out_specs=(vmem, vmem),
        scratch_shapes=[
            pltpu.VMEM(bins.shape, F32),
            pltpu.VMEM(block, F32),
            pltpu.VMEM(block, F32),
            pltpu.VMEM(block, F32),
            pltpu.VMEM((4,) + block, F32),
            pltpu.VMEM((2, groups, CLON, CLAT), F32),
            pltpu.VMEM((2, STEPS, levels, CLAT), F32),
            pltpu.VMEM((2, STEPS, levels, CLAT), F32),
            pltpu.VMEM((2, STEPS, groups, CLON, CLAT), F32),
            pltpu.VMEM((2, STEPS, groups, CLON, CLAT), F32),
            pltpu.SemaphoreType.DMA((STEPS,)),
            pltpu.SemaphoreType.DMA((STEPS,)),
            pltpu.SemaphoreType.DMA((4, STEPS)),
            pltpu.SemaphoreType.DMA((4, STEPS)),
        ],
        compiler_params=pltpu.CompilerParams(
            collective_id=0, has_side_effects=True, vmem_limit_bytes=VMEM_LIMIT),
    )(bins, horizontal, vertical)


def per_device(kernel, residual, owner_block, column, time_step, horizontal, vertical):
    owners = lax.axis_size("lon") * lax.axis_size("lat")
    capacity = 4 * kernel.shape[1] // owners
    slots = pack(kernel, residual, owner_block, column, time_step, owners, capacity)
    return transport(bin_soundings(slots, kernel.shape[0]), horizontal, vertical)


def solution(mesh):
    placed = (
        P(None, ("orbit", "lon", "lat")),
        P(("orbit", "lon", "lat")),
        P(("orbit", "lon", "lat"), None),
        P(("orbit", "lon", "lat")),
        P(("orbit", "lon", "lat")),
        P(None, None, "lon", "lat"),
        P(None, "lon", "lat"),
    )
    return jax.shard_map(
        per_device,
        mesh=mesh,
        in_specs=placed,
        out_specs=(P(None, "lon", "lat"), P("lon", "lat")),
        check_vma=False,
    )
```
